256 devices in a mesh: ta: 8 (over z_lo, core), col: 32 (over x, y, z_hi).
Axes of the slice: x: 4, y: 4, z: 8 (z_hi: 2, z_lo: 4; z = z_hi * 4 + z_lo), core: 2. Of those that a mesh axis runs over, the one named last changes fastest.
Arguments:
- voltages: bfloat16 [2048, 1024, 128], P('ta', 'col'), may hold values from -6 to 6
- taps_filter: float32 [16, 128], replicated, may hold values from -0.125 to 0.125
Outputs:
- spectra: bfloat16 [64, 2, 2048, 1024], P('col', None, 'ta')
- visibilities: float32 [1024, 64, 2, 1024], P('ta', 'col')
The draws below stay inside these ranges and needn't reach their ends.
All inputs are finite; a program needn't handle non-finite values.
Results may differ from the reference program's by a relative error of at most 0.015.
Values may be sent and summed in bfloat16 or wider, within the bound.
A program may use at most 128 MiB of HBM per device.

```python
import jax
import jax.numpy as jnp
from jax import lax

NIN = 1024
CH = 64
FR = 128
TAPS = 16
FRAMES_DEV = 256
FRAMES = 2048
N_TA = 8


def block_scale(key, shape, pieces, smallest, largest):
    loudness = 1.0
    for position, parts in pieces:
        steps = jax.random.uniform(jax.random.fold_in(jax.random.fold_in(key, 6), position), (parts,), jnp.float32, smallest / len(pieces), largest / len(pieces))
        loudness = loudness * jnp.repeat(jnp.exp(steps), shape[position] // parts).reshape((-1,) + (1,) * (len(shape) - 1 - position))
    return loudness


def noise(rng, dims, spread, limit, shards=(), kind=jnp.bfloat16):
    entries = jax.random.normal(rng, dims, jnp.float32) * spread
    if len(shards) > 0:
        entries = block_scale(rng, dims, shards, -0.22, 0.18) * entries
    return jnp.clip(entries, min=-limit, max=limit).astype(kind)


def setup_inputs(seed: int = 0) -> dict:
    arg_keys = jax.random.split(jax.random.key(seed), 3)
    voltages = noise(arg_keys[0], (FRAMES, NIN, FR), 1.0, 6.0, ((0, 8), (1, 32)))
    taps_filter = noise(arg_keys[1], (TAPS, FR), (TAPS * FR) ** -0.5, 0.125, (), jnp.float32)
    return dict(voltages=voltages, taps_filter=taps_filter)


def make_table(width, chans):
    samples = jnp.arange(width, dtype=jnp.int32)
    freqs = jnp.arange(chans, dtype=jnp.int32)
    phase = ((samples[:, None] * freqs[None, :]) % width).astype(jnp.float32)
    angle = 2.0 * jnp.pi * phase / width
    return jnp.concatenate([jnp.cos(angle), -jnp.sin(angle)], axis=1).astype(jnp.bfloat16)


def reference(voltages, taps_filter):
    table = make_table(FR, CH)
    width_block = NIN // 16
    blocks = jnp.moveaxis(voltages.reshape(FRAMES, 16, width_block, FR), 1, 0)

    def front(block):
        padded = jnp.concatenate([jnp.zeros((TAPS - 1, width_block, FR), jnp.bfloat16), block], axis=0).astype(jnp.float32)
        total = jnp.zeros((FRAMES, width_block, FR), jnp.float32)
        for tap in range(TAPS):
            total = total + taps_filter[tap][None, None, :] * padded[tap:tap + FRAMES]
        filtered = total.astype(jnp.bfloat16)
        spec = jnp.dot(filtered.reshape(FRAMES * width_block, FR), table, preferred_element_type=jnp.float32)
        return spec.astype(jnp.bfloat16).reshape(FRAMES, width_block, 2, CH)

    specs = lax.map(front, blocks)
    spectra = jnp.transpose(specs, (4, 3, 1, 0, 2)).reshape(CH, 2, FRAMES, NIN)

    def correlate(channel):
        groups = jnp.transpose(channel.reshape(2, N_TA, FRAMES_DEV, NIN), (1, 0, 2, 3))

        def step(total, group):
            real_a = group[0]
            imag_b = group[1]
            real_part = jnp.dot(real_a.T, real_a, preferred_element_type=jnp.float32) + jnp.dot(imag_b.T, imag_b, preferred_element_type=jnp.float32)
            imag_part = jnp.dot(real_a.T, imag_b, preferred_element_type=jnp.float32) - jnp.dot(imag_b.T, real_a, preferred_element_type=jnp.float32)
            part = (jnp.stack([real_part, imag_part]) * (1.0 / FRAMES)).astype(jnp.bfloat16)
            part = lax.optimization_barrier(part)
            return total + part.astype(jnp.float32), None

        total, unused = lax.scan(step, jnp.zeros((2, NIN, NIN), jnp.float32), groups)
        return total

    visib = lax.map(correlate, spectra)
    return spectra, jnp.transpose(visib, (2, 0, 1, 3))
```

```python
import jax
import jax.numpy as jnp
import numpy as np
from jax import lax
from jax.experimental import pallas as pl
from jax.experimental.pallas import tpu as pltpu
from jax.sharding import PartitionSpec as P

MESH = pl.DeviceIdType.MESH
F32 = jnp.float32
BF16 = jnp.bfloat16

TAPS = 16
FR = 128
FRAMES = 256
LOCAL = 32
COLS = 32
NIN = 1024
CHIPS = 4
BLK = NIN // CHIPS
QF = FRAMES // 4
JC = 16
NJC = QF // JC
GROUPS = COLS // 4

ORDER = [(i, j) for j in range(CHIPS - 1, -1, -1) for i in range(j + 1)]


def make_table_rows():
    samples = np.arange(FR)
    chans = np.arange(FR // 2)
    angle = 2.0 * np.pi * ((chans[:, None] * samples[None, :]) % FR) / FR
    both = np.stack([np.cos(angle), -np.sin(angle)], axis=1)
    return jnp.asarray(both.reshape(FR, FR), F32).astype(BF16)


def make_regroup():
    perm = np.zeros((4, 4, LOCAL, 4, 4, LOCAL), np.float32)
    for i in range(4):
        for b in range(4):
            for n in range(LOCAL):
                perm[i, b, n, b, i, n] = 1.0
    return jnp.asarray(perm.reshape(512, 512), BF16)


def kernel(
    volt, taps, table, regroup, spec_out, vis_out,
    padded, filt, wide, sendbuf, recvbuf, spec, gram, turned, part, outgo_a, outgo_b, from_out, from_in, halves, halves_in,
    load_sem, halo_sem, a2a_send, a2a_recv, own_sem, pair_sem, line_send, line_recv, half_sem, out_sem,
):
    ta = lax.axis_index("ta")
    col = lax.axis_index("col")
    chip = ta // 2
    core = ta % 2
    mirror = chip // 2
    middle = chip * (1 - mirror) + (3 - chip) * mirror
    inner = {"ta": (chip + 1 - 2 * mirror) * 2 + core, "col": col}
    outer = {"ta": (chip - 1 + 2 * mirror) * 2 + core, "col": col}
    sibling = {"ta": chip * 2 + 1 - core, "col": col}
    before = {"ta": ta - 1, "col": col}
    after = {"ta": ta + 1, "col": col}
    is_end = middle == 0
    is_middle = middle == 1
    cross_after = jnp.logical_and(core == 1, chip < CHIPS - 1)
    cross_before = jnp.logical_and(core == 0, chip > 0)

    load = pltpu.make_async_copy(volt, padded.at[pl.ds(TAPS, FRAMES)], load_sem.at[0])
    load.start()

    barrier = pltpu.get_barrier_semaphore()

    def greet(device):
        pl.semaphore_signal(barrier, inc=1, device_id=device, device_id_type=MESH)

    def greet_col(step, carry):
        greet({"ta": ta, "col": (col + step) % COLS})
        return carry

    lax.fori_loop(1, COLS, greet_col, 0)
    greet(sibling)
    greet(inner)

    @pl.when(is_middle)
    def _():
        greet(outer)

    @pl.when(cross_after)
    def _():
        greet(after)

    @pl.when(cross_before)
    def _():
        greet(before)

    @pl.when(ta == 0)
    def _():
        padded[0:TAPS] = jnp.zeros((TAPS, LOCAL, FR), BF16)

    load.wait()

    def front(chunk):
        def filter_part(step, carry):
            group = step // 2
            rows = pl.ds(pl.multiple_of((step % 2) * 16, 16), 16)
            out_rows = pl.ds(pl.multiple_of(group * LOCAL + (step % 2) * 16, 16), 16)
            weights = [taps[t : t + 1, :] for t in range(TAPS)]
            for part_of in range(JC // 8):
                base = group * QF + chunk * JC + part_of * 8 + 1
                held = [padded[base + i, rows, :].astype(F32) for i in range(TAPS + 7)]
                for o in range(8):
                    total = weights[0] * held[o]
                    for t in range(1, TAPS):
                        total = total + weights[t] * held[o + t]
                    filt[part_of * 8 + o, out_rows, :] = total.astype(BF16)
            return carry

        lax.fori_loop(0, 8, filter_part, 0)
        for j in range(JC):
            wide[pl.ds(j, FR, stride=JC), :] = lax.dot_general(
                table[...], filt[j], (((1,), (1,)), ((), ())), preferred_element_type=F32
            )
        sendbuf[:, pl.ds(chunk * JC, JC), :] = wide[...].reshape(FR, JC, FR).astype(BF16)

    def send_chunk(chunk):
        rows = pl.ds(chunk * JC, JC)

        def send_one(step, carry):
            peer = (col + step) % COLS
            pltpu.make_async_remote_copy(
                src_ref=sendbuf.at[pl.ds(peer * 4, 4), rows],
                dst_ref=recvbuf.at[col, :, rows],
                send_sem=a2a_send.at[peer],
                recv_sem=a2a_recv.at[col],
                device_id={"ta": ta, "col": peer},
                device_id_type=MESH,
            ).start()
            return carry

        lax.fori_loop(1, COLS, send_one, 0)

    halo = pltpu.make_async_remote_copy(
        src_ref=padded.at[pl.ds(FRAMES, TAPS)],
        dst_ref=padded.at[pl.ds(0, TAPS)],
        send_sem=halo_sem.at[0],
        recv_sem=halo_sem.at[1],
        device_id=after,
        device_id_type=MESH,
    )

    front(1)
    pl.semaphore_wait(
        barrier,
        COLS + 1 + middle + cross_after.astype(jnp.int32) + cross_before.astype(jnp.int32),
    )

    @pl.when(ta < 2 * CHIPS - 1)
    def _():
        halo.start()

    send_chunk(1)
    front(2)
    send_chunk(2)
    front(3)
    send_chunk(3)

    @pl.when(ta > 0)
    def _():
        halo.wait_recv()

    front(0)
    send_chunk(0)
    own = pltpu.make_async_copy(sendbuf.at[pl.ds(col * 4, 4)], recvbuf.at[col], own_sem.at[0])
    own.start()
    own.wait()

    def regroup_one(g, carry):
        lanes = pl.ds(pl.multiple_of(g * 128, 128), 128)
        for i in range(4):
            source = g * 4 + i

            @pl.when(source != col)
            def _():
                pltpu.make_async_remote_copy(
                    src_ref=recvbuf.at[source],
                    dst_ref=recvbuf.at[source],
                    send_sem=a2a_send.at[source],
                    recv_sem=a2a_recv.at[source],
                    device_id={"ta": ta, "col": source},
                    device_id_type=MESH,
                ).wait_recv()

        total = jnp.zeros((4 * QF, 512), F32)
        for i in range(4):
            total = total + jnp.dot(
                recvbuf[g * 4 + i].reshape(4 * QF, FR),
                regroup[i * 128 : (i + 1) * 128, :],
                preferred_element_type=F32,
            )
        for b in range(4):
            spec[:, b * QF : (b + 1) * QF, lanes] = (
                total[:, b * 128 : (b + 1) * 128].astype(BF16).reshape(4, QF, 128)
            )
        pltpu.make_async_remote_copy(
            src_ref=spec.at[pl.ds(2 * (1 - core), 2), :, lanes],
            dst_ref=gram.at[:, :, lanes],
            send_sem=pair_sem.at[0],
            recv_sem=pair_sem.at[1],
            device_id=sibling,
            device_id_type=MESH,
        ).start()
        return carry

    lax.fori_loop(0, GROUPS, regroup_one, 0)
    write_spec = pltpu.make_async_copy(spec, spec_out, out_sem.at[0])
    write_spec.start()
    pair = pltpu.make_async_remote_copy(
        src_ref=spec.at[pl.ds(2 * (1 - core), 2)],
        dst_ref=gram,
        send_sem=pair_sem.at[0],
        recv_sem=pair_sem.at[1],
        device_id=sibling,
        device_id_type=MESH,
    )
    pair.wait_recv()

    def actual(i, j):
        return i + mirror * (3 - i - j), j + mirror * (3 - i - j)

    def planes_of(i, j):
        return 1 if i == j else 2

    def slot_of(i, j):
        rows, columns = actual(i, j)
        return rows * CHIPS + columns

    def stream(buffer, landing, i, j, channel, device):
        slot = slot_of(i, j)
        planes = pl.ds(0, planes_of(i, j))
        return pltpu.make_async_remote_copy(
            src_ref=buffer.at[slot, planes],
            dst_ref=landing.at[slot, planes],
            send_sem=line_send.at[channel, slot],
            recv_sem=line_recv.at[channel, slot],
            device_id=device,
            device_id_type=MESH,
        )

    own_real = 2 * core
    turned[0:256, :] = spec[own_real + 1]
    turned[256:512, :] = -spec[own_real]
    turned[512:768, :] = gram[1]
    turned[768:1024, :] = -gram[0]

    row_id = lax.broadcasted_iota(jnp.int32, (BLK, BLK), 0)
    col_id = lax.broadcasted_iota(jnp.int32, (BLK, BLK), 1)

    for i, j in ORDER:
        rows, columns = actual(i, j)
        left = pl.ds(pl.multiple_of(rows * BLK, BLK), BLK)
        right = pl.ds(pl.multiple_of(columns * BLK, BLK), BLK)
        slot = slot_of(i, j)
        lhs = jnp.concatenate(
            [spec[own_real, :, left], spec[own_real + 1, :, left], gram[0, :, left], gram[1, :, left]], axis=0
        )
        rhs = jnp.concatenate(
            [spec[own_real, :, right], spec[own_real + 1, :, right], gram[0, :, right], gram[1, :, right]], axis=0
        )
        dims = (((0,), (0,)), ((), ()))
        real = lax.dot_general(lhs, rhs, dims, preferred_element_type=F32)
        imag = lax.dot_general(lhs, turned[:, right], dims, preferred_element_type=F32)
        if i == j:
            part[slot, 0] = jnp.where(row_id <= col_id, real, imag)
        else:
            part[slot, 0] = real
            part[slot, 1] = imag
        if j >= 1:

            @pl.when(is_end)
            def _():
                for plane in range(planes_of(i, j)):
                    outgo_a[slot, plane] = part[slot, plane].astype(BF16)
                stream(outgo_a, from_out, i, j, 0, inner).start()

    inward = [(i, j) for i, j in ORDER if j >= 2]
    outward = [(0, j) for j in range(CHIPS - 1, -1, -1)]

    @pl.when(is_middle)
    def _():
        for step in range(len(inward)):
            i, j = inward[step]
            slot = slot_of(i, j)
            stream(outgo_a, from_out, i, j, 0, outer).wait_recv()
            for plane in range(planes_of(i, j)):
                outgo_a[slot, plane] = (part[slot, plane] + from_out[slot, plane].astype(F32)).astype(BF16)
            stream(outgo_a, from_in, i, j, 1, inner).start()
            if step < len(outward):
                i, j = outward[step]
                slot = slot_of(i, j)
                stream(outgo_b, from_in, i, j, 1, inner).wait_recv()
                for plane in range(planes_of(i, j)):
                    outgo_b[slot, plane] = (part[slot, plane] + from_in[slot, plane].astype(F32)).astype(BF16)
                stream(outgo_b, from_in, i, j, 2, outer).start()

    scale = 1.0 / (FRAMES * 2 * CHIPS)

    def finish(i, j, own_is_row, total):
        rows, columns = actual(i, j)
        if i == j:
            lanes = pl.ds(pl.multiple_of(rows * BLK, BLK), BLK)
            packed = total(0)
            flipped = packed.T
            real = jnp.where(row_id <= col_id, packed, flipped)
            imag = jnp.where(row_id > col_id, packed, jnp.where(row_id == col_id, 0.0, -flipped))
            for h in range(2):
                halves[h, 0, :, lanes] = real[h * 128 : (h + 1) * 128] * scale
                halves[h, 1, :, lanes] = imag[h * 128 : (h + 1) * 128] * scale
        else:
            straight = mirror == (0 if own_is_row else 1)

            @pl.when(straight)
            def _():
                lanes = pl.ds(pl.multiple_of(columns * BLK, BLK), BLK)
                for plane in range(2):
                    value = total(plane) * scale
                    for h in range(2):
                        halves[h, plane, :, lanes] = value[h * 128 : (h + 1) * 128]

            @pl.when(jnp.logical_not(straight))
            def _():
                lanes = pl.ds(pl.multiple_of(rows * BLK, BLK), BLK)
                for plane in range(2):
                    value = total(plane).T * (scale if plane == 0 else -scale)
                    for h in range(2):
                        halves[h, plane, :, lanes] = value[h * 128 : (h + 1) * 128]

    @pl.when(is_end)
    def _():
        for i, j in outward:
            slot = slot_of(i, j)
            stream(outgo_b, from_in, i, j, 2, inner).wait_recv()
            finish(i, j, True, lambda plane: part[slot, plane] + from_in[slot, plane].astype(F32))

    @pl.when(is_middle)
    def _():
        for i, j in [(1, 3), (1, 2), (0, 1), (1, 1)]:
            slot = slot_of(i, j)
            if j == 1:
                stream(outgo_a, from_out, i, j, 0, outer).wait_recv()
            if i == 1:
                stream(outgo_a, from_in, i, j, 1, inner).wait_recv()
            finish(
                i, j, i == 1,
                lambda plane: part[slot, plane] + from_out[slot, plane].astype(F32) + from_in[slot, plane].astype(F32),
            )

    swap = pltpu.make_async_remote_copy(
        src_ref=halves.at[1 - core],
        dst_ref=halves_in,
        send_sem=half_sem.at[0],
        recv_sem=half_sem.at[1],
        device_id=sibling,
        device_id_type=MESH,
    )
    swap.start()
    write_own = pltpu.make_async_copy(halves.at[core], vis_out.at[core], out_sem.at[1])
    write_own.start()
    swap.wait_recv()
    write_other = pltpu.make_async_copy(halves_in, vis_out.at[1 - core], out_sem.at[2])
    write_other.start()

    swap.wait_send()
    pair.wait_send()

    @pl.when(ta < 2 * CHIPS - 1)
    def _():
        halo.wait_send()

    def drain(step, carry):
        peer = (col + step) % COLS
        pltpu.make_async_remote_copy(
            src_ref=sendbuf.at[pl.ds(peer * 4, 4)],
            dst_ref=recvbuf.at[col],
            send_sem=a2a_send.at[peer],
            recv_sem=a2a_recv.at[col],
            device_id={"ta": ta, "col": peer},
            device_id_type=MESH,
        ).wait_send()
        return carry

    lax.fori_loop(1, COLS, drain, 0)

    @pl.when(is_end)
    def _():
        for i, j in ORDER:
            if j >= 1:
                stream(outgo_a, from_out, i, j, 0, inner).wait_send()

    @pl.when(is_middle)
    def _():
        for i, j in inward:
            stream(outgo_a, from_in, i, j, 1, inner).wait_send()
        for i, j in outward:
            stream(outgo_b, from_in, i, j, 2, outer).wait_send()

    write_spec.wait()
    write_own.wait()
    write_other.wait()


def body(voltages, taps_filter):
    blocks = (CHIPS * CHIPS, 2, BLK, BLK)
    spectra, visib = pl.pallas_call(
        kernel,
        out_shape=(
            jax.ShapeDtypeStruct((4, FRAMES, NIN), BF16),
            jax.ShapeDtypeStruct((2, 2, 128, NIN), F32),
        ),
        in_specs=[
            pl.BlockSpec(memory_space=pl.ANY),
            pl.BlockSpec(memory_space=pltpu.VMEM),
            pl.BlockSpec(memory_space=pltpu.VMEM),
            pl.BlockSpec(memory_space=pltpu.VMEM),
        ],
        out_specs=(pl.BlockSpec(memory_space=pl.ANY), pl.BlockSpec(memory_space=pl.ANY)),
        scratch_shapes=[
            pltpu.VMEM((FRAMES + TAPS, LOCAL, FR), BF16),
            pltpu.VMEM((JC, FR, FR), BF16),
            pltpu.VMEM((JC * FR, FR), F32),
            pltpu.VMEM((FR, QF, FR), BF16),
            pltpu.VMEM((COLS, 4, QF, FR), BF16),
            pltpu.VMEM((4, FRAMES, NIN), BF16),
            pltpu.VMEM((2, FRAMES, NIN), BF16),
            pltpu.VMEM((4 * FRAMES, NIN), BF16),
            pltpu.VMEM(blocks, F32),
            pltpu.VMEM(blocks, BF16),
            pltpu.VMEM(blocks, BF16),
            pltpu.VMEM(blocks, BF16),
            pltpu.VMEM(blocks, BF16),
            pltpu.VMEM((2, 2, 128, NIN), F32),
            pltpu.VMEM((2, 128, NIN), F32),
            pltpu.SemaphoreType.DMA((1,)),
            pltpu.SemaphoreType.DMA((2,)),
            pltpu.SemaphoreType.DMA((COLS,)),
            pltpu.SemaphoreType.DMA((COLS,)),
            pltpu.SemaphoreType.DMA((1,)),
            pltpu.SemaphoreType.DMA((2,)),
            pltpu.SemaphoreType.DMA((3, CHIPS * CHIPS)),
            pltpu.SemaphoreType.DMA((3, CHIPS * CHIPS)),
            pltpu.SemaphoreType.DMA((2,)),
            pltpu.SemaphoreType.DMA((3,)),
        ],
        compiler_params=pltpu.CompilerParams(
            collective_id=0, has_side_effects=True, vmem_limit_bytes=60 * 2**20
        ),
        name="correlator",
    )(voltages, taps_filter, make_table_rows(), make_regroup())
    return spectra.reshape(2, 2, FRAMES, NIN), jnp.transpose(visib, (2, 0, 1, 3))


def solution(mesh):
    return jax.shard_map(
        body,
        mesh=mesh,
        in_specs=(P("ta", "col", None), P()),
        out_specs=(P("col", None, "ta", None), P("ta", "col", None, None)),
        check_vma=False,
    )
```

```python
import jax
import jax.numpy as jnp
import numpy as np
from jax import lax
from jax.experimental import pallas as pl
from jax.experimental.pallas import tpu as pltpu
from jax.sharding import PartitionSpec as P

MESH = pl.DeviceIdType.MESH
F32 = jnp.float32
BF16 = jnp.bfloat16

TAPS = 16
FR = 128
FRAMES = 256
LOCAL = 32
COLS = 32
NIN = 1024
CHIPS = 4
BLK = NIN // CHIPS
QF = FRAMES // 4
JC = 16
NJC = QF // JC
GROUPS = COLS // 4

ORDER = [(i, j) for j in range(CHIPS - 1, -1, -1) for i in range(j + 1)]


def make_table_rows():
    samples = np.arange(FR)
    chans = np.arange(FR // 2)
    angle = 2.0 * np.pi * ((chans[:, None] * samples[None, :]) % FR) / FR
    both = np.stack([np.cos(angle), -np.sin(angle)], axis=1)
    return jnp.asarray(both.reshape(FR, FR), F32).astype(BF16)


def kernel(
    volt, taps, table, spec_out, vis_out,
    padded, filt, wide, sendbuf, recvbuf, spectra, across, right, for_sibling, part, outgo_a, outgo_b, from_out, from_in, work, stage, arrived, rows_out,
    load_sem, halo_sem, a2a_send, a2a_recv, own_sem, pair_send, pair_recv, line_send, line_recv, half_send, half_recv, out_sem,
):
    ta = lax.axis_index("ta")
    col = lax.axis_index("col")
    chip = ta // 2
    core = ta % 2
    mirror = chip // 2
    middle = chip * (1 - mirror) + (3 - chip) * mirror
    inner = {"ta": (chip + 1 - 2 * mirror) * 2 + core, "col": col}
    outer = {"ta": (chip - 1 + 2 * mirror) * 2 + core, "col": col}
    sibling = {"ta": chip * 2 + 1 - core, "col": col}
    before = {"ta": ta - 1, "col": col}
    after = {"ta": ta + 1, "col": col}
    is_end = middle == 0
    is_middle = middle == 1
    cross_after = jnp.logical_and(core == 1, chip < CHIPS - 1)
    cross_before = jnp.logical_and(core == 0, chip > 0)

    load = pltpu.make_async_copy(volt, padded.at[pl.ds(TAPS, FRAMES)], load_sem.at[0])
    load.start()

    barrier = pltpu.get_barrier_semaphore()

    def greet(device):
        pl.semaphore_signal(barrier, inc=1, device_id=device, device_id_type=MESH)

    def greet_col(step, carry):
        greet({"ta": ta, "col": (col + step) % COLS})
        return carry

    lax.fori_loop(1, COLS, greet_col, 0)
    greet(sibling)
    greet(inner)

    @pl.when(is_middle)
    def _():
        greet(outer)

    @pl.when(cross_after)
    def _():
        greet(after)

    @pl.when(cross_before)
    def _():
        greet(before)

    @pl.when(ta == 0)
    def _():
        padded[0:TAPS] = jnp.zeros((TAPS, LOCAL, FR), BF16)

    load.wait()

    def front(chunk):
        def filter_part(step, carry):
            group = step // 2
            rows = pl.ds(pl.multiple_of((step % 2) * 16, 16), 16)
            out_rows = pl.ds(pl.multiple_of(group * LOCAL + (step % 2) * 16, 16), 16)
            weights = [taps[t : t + 1, :] for t in range(TAPS)]
            for part_of in range(JC // 8):
                base = group * QF + chunk * JC + part_of * 8 + 1
                held = [padded[base + i, rows, :].astype(F32) for i in range(TAPS + 7)]
                for o in range(8):
                    total = weights[0] * held[o]
                    for t in range(1, TAPS):
                        total = total + weights[t] * held[o + t]
                    filt[part_of * 8 + o, out_rows, :] = total.astype(BF16)
            return carry

        lax.fori_loop(0, 8, filter_part, 0)
        for j in range(JC):
            wide[pl.ds(j, FR, stride=JC), :] = lax.dot_general(
                table[...], filt[j], (((1,), (1,)), ((), ())), preferred_element_type=F32
            )
        sendbuf[:, pl.ds(chunk * JC, JC), :] = wide[...].reshape(FR, JC, FR).astype(BF16)

    def to_owner(channel, peer, rows):
        return pltpu.make_async_remote_copy(
            src_ref=sendbuf.at[pl.ds(peer * 4 + 2 * channel, 2), rows],
            dst_ref=recvbuf.at[col, pl.ds(2 * channel, 2), rows],
            send_sem=a2a_send.at[channel, peer],
            recv_sem=a2a_recv.at[channel, col],
            device_id={"ta": ta, "col": peer},
            device_id_type=MESH,
        )

    def send_chunk(channel, rows):
        def send_one(step, carry):
            to_owner(channel, (col + step) % COLS, rows).start()
            return carry

        lax.fori_loop(1, COLS, send_one, 0)

    halo = pltpu.make_async_remote_copy(
        src_ref=padded.at[pl.ds(FRAMES, TAPS)],
        dst_ref=padded.at[pl.ds(0, TAPS)],
        send_sem=halo_sem.at[0],
        recv_sem=halo_sem.at[1],
        device_id=after,
        device_id_type=MESH,
    )

    front(1)
    pl.semaphore_wait(
        barrier,
        COLS + 1 + middle + cross_after.astype(jnp.int32) + cross_before.astype(jnp.int32),
    )

    @pl.when(ta < 2 * CHIPS - 1)
    def _():
        halo.start()

    send_chunk(0, pl.ds(1 * JC, JC))
    front(2)
    send_chunk(0, pl.ds(2 * JC, JC))
    front(3)
    send_chunk(0, pl.ds(3 * JC, JC))

    @pl.when(ta > 0)
    def _():
        halo.wait_recv()

    front(0)
    send_chunk(0, pl.ds(0 * JC, JC))
    send_chunk(1, pl.ds(0, QF))
    own = pltpu.make_async_copy(sendbuf.at[pl.ds(col * 4, 4)], recvbuf.at[col], own_sem.at[0])
    own.start()
    own.wait()

    def pair_copies(channel, lanes):
        own_k, sibling_k = pl.ds(0, 2 * FRAMES), pl.ds(2 * FRAMES, 2 * FRAMES)
        ways = [
            (across.at[channel, lanes, own_k], across.at[channel, lanes, sibling_k]),
            (for_sibling.at[channel, :, lanes], right.at[channel, sibling_k, lanes]),
        ]
        return [
            pltpu.make_async_remote_copy(
                src_ref=src,
                dst_ref=dst,
                send_sem=pair_send.at[channel, way],
                recv_sem=pair_recv.at[channel, way],
                device_id=sibling,
                device_id_type=MESH,
            )
            for way, (src, dst) in enumerate(ways)
        ]

    def gather(channel):
        def regroup_one(g, carry):
            lanes = pl.ds(pl.multiple_of(g * 128, 128), 128)
            for i in range(4):
                source = g * 4 + i

                @pl.when(source != col)
                def _():
                    pltpu.make_async_remote_copy(
                        src_ref=recvbuf.at[source, pl.ds(2 * channel, 2)],
                        dst_ref=recvbuf.at[source, pl.ds(2 * channel, 2)],
                        send_sem=a2a_send.at[channel, source],
                        recv_sem=a2a_recv.at[channel, source],
                        device_id={"ta": ta, "col": source},
                        device_id_type=MESH,
                    ).wait_recv()

            for r in range(2):
                held = [recvbuf[g * 4 + i, 2 * channel + r] for i in range(4)]
                value = jnp.concatenate(
                    [
                        jnp.concatenate([h[:, b * LOCAL : (b + 1) * LOCAL] for h in held], axis=1)
                        for b in range(4)
                    ],
                    axis=0,
                )
                here, there = pl.ds(r * FRAMES, FRAMES), pl.ds((1 - r) * FRAMES, FRAMES)
                spectra[channel, here, lanes] = value
                across[channel, lanes, here] = value.T

                @pl.when(core == 0)
                def _():
                    right[channel, here, lanes] = value
                    for_sibling[channel, there, lanes] = value if r == 1 else -value

                @pl.when(core == 1)
                def _():
                    right[channel, there, lanes] = value if r == 1 else -value
                    for_sibling[channel, here, lanes] = value

            for copy in pair_copies(channel, lanes):
                copy.start()
            return carry

        lax.fori_loop(0, GROUPS, regroup_one, 0)

    def spec_copy(channel):
        return pltpu.make_async_copy(spectra.at[channel], spec_out.at[channel], out_sem.at[channel])

    def actual(i, j):
        return i + mirror * (3 - i - j), j + mirror * (3 - i - j)

    def slot_of(i, j):
        rows, columns = actual(i, j)
        return columns * (columns + 1) // 2 + rows

    def lanes_of(block):
        return pl.ds(pl.multiple_of(block * BLK, BLK), BLK)

    def mine(i, j):
        return None if i != j else core == (i + mirror) % 2

    def if_mine(i, j, run):
        if i == j:
            pl.when(mine(i, j))(run)
        else:
            run()

    def stream(buffer, landing, channel, i, j, way, device):
        slot = slot_of(i, j)
        return pltpu.make_async_remote_copy(
            src_ref=buffer.at[channel, slot],
            dst_ref=landing.at[channel, slot],
            send_sem=line_send.at[channel, way, slot],
            recv_sem=line_recv.at[channel, way, slot],
            device_id=device,
            device_id_type=MESH,
        )


    row_id = lax.broadcasted_iota(jnp.int32, (BLK, BLK), 0)
    col_id = lax.broadcasted_iota(jnp.int32, (BLK, BLK), 1)
    inward = [(i, j) for i, j in ORDER if j >= 2]
    outward = [(0, j) for j in range(CHIPS - 1, -1, -1)]
    forwards = {
        (0, 3): [("in", 0, 3)],
        (1, 3): [("in", 1, 3)],
        (2, 3): [("in", 2, 3)],
        (3, 3): [("in", 3, 3), ("out", 0, 3)],
        (0, 2): [("out", 0, 2)],
        (0, 1): [("out", 0, 1)],
        (0, 0): [("out", 0, 0), ("in", 0, 2), ("in", 1, 2), ("in", 2, 2)],
    }

    def product(channel, i, j):
        rows, columns = actual(i, j)
        slot = slot_of(i, j)
        lhs = across[channel, lanes_of(rows), :]
        value = jnp.dot(lhs, right[channel, :, lanes_of(columns)], preferred_element_type=F32)
        if i == j:
            other = jnp.zeros((BLK, BLK), F32)
            for k in range(4):
                term = jnp.dot(
                    lhs[:, k * FRAMES : (k + 1) * FRAMES],
                    right[channel, (k ^ 1) * FRAMES : ((k ^ 1) + 1) * FRAMES, lanes_of(columns)],
                    preferred_element_type=F32,
                )
                other = other + term if k % 2 == 0 else other - term
            real = jnp.where(core == 0, value, -other)
            imag = jnp.where(core == 0, other, value)
            value = jnp.where(row_id <= col_id, real, imag)
        part[channel, slot] = value
        if j >= 1:

            @pl.when(is_end)
            def _():
                outgo_a[channel, slot] = value.astype(BF16)
                stream(outgo_a, from_out, channel, i, j, 0, inner).start()

    def to_inner(channel, i, j):
        slot = slot_of(i, j)
        stream(outgo_a, from_out, channel, i, j, 0, outer).wait_recv()
        outgo_a[channel, slot] = (part[channel, slot] + from_out[channel, slot].astype(F32)).astype(BF16)
        stream(outgo_a, from_in, channel, i, j, 1, inner).start()

    def to_outer(channel, i, j):
        slot = slot_of(i, j)
        stream(outgo_b, from_in, channel, i, j, 1, inner).wait_recv()
        outgo_b[channel, slot] = (part[channel, slot] + from_in[channel, slot].astype(F32)).astype(BF16)
        stream(outgo_b, from_in, channel, i, j, 2, outer).start()

    def products(channel):
        for i, j in ORDER:
            if_mine(i, j, lambda: product(channel, i, j))

            if (i, j) in forwards:

                @pl.when(is_middle)
                def _():
                    for way, k, l in forwards[i, j]:
                        if_mine(k, l, lambda: (to_inner if way == "in" else to_outer)(channel, k, l))

    scale = 1.0 / (FRAMES * 2 * CHIPS)

    def swap(channel, block, planes):
        return pltpu.make_async_remote_copy(
            src_ref=stage.at[channel, planes, :, lanes_of(block)],
            dst_ref=arrived.at[channel, planes, :, lanes_of(block)],
            send_sem=half_send.at[channel, block],
            recv_sem=half_recv.at[channel, block],
            device_id=sibling,
            device_id_type=MESH,
        )

    def put(channel, block, plane, value):
        rows_out[:, channel, plane, lanes_of(block)] = value

    own_rows = pl.ds(pl.multiple_of(core * 128, 128), 128)
    other_rows = pl.ds(pl.multiple_of((1 - core) * 128, 128), 128)

    def finish_block(channel, i, j, own_is_row, total):
        rows, columns = actual(i, j)
        if i == j:

            @pl.when(mine(i, j))
            def _():
                packed = total() * scale
                flipped = packed.T
                work[0] = jnp.where(row_id <= col_id, packed, flipped)
                work[1] = jnp.where(row_id > col_id, packed, jnp.where(row_id == col_id, 0.0, -flipped))
                for plane in range(2):
                    stage[channel, plane, :, lanes_of(rows)] = work[plane, other_rows, :]
                swap(channel, rows, pl.ds(0, 2)).start()
                for plane in range(2):
                    put(channel, rows, plane, work[plane, own_rows, :])

        else:
            straight = mirror == (0 if own_is_row else 1)
            block = columns * straight.astype(jnp.int32) + rows * (1 - straight.astype(jnp.int32))

            @pl.when(straight)
            def _():
                work[0] = total() * scale

            @pl.when(jnp.logical_not(straight))
            def _():
                work[0] = total().T * (scale * (1 - 2 * core).astype(F32))

            stage[channel, core, :, lanes_of(block)] = work[0, other_rows, :]
            swap(channel, block, pl.ds(core, 1)).start()
            put(channel, block, core, work[0, own_rows, :])

    def finish(channel):
        @pl.when(is_end)
        def _():
            for i, j in outward:
                slot = slot_of(i, j)

                def wait(i=i, j=j):
                    stream(outgo_b, from_in, channel, i, j, 2, inner).wait_recv()

                if_mine(i, j, wait)
                finish_block(
                    channel, i, j, True, lambda: part[channel, slot] + from_in[channel, slot].astype(F32)
                )

        @pl.when(is_middle)
        def _():
            for i, j in [(1, 3), (1, 2), (0, 1), (1, 1)]:
                slot = slot_of(i, j)

                def wait(i=i, j=j):
                    if j == 1:
                        stream(outgo_a, from_out, channel, i, j, 0, outer).wait_recv()
                    if i == 1:
                        stream(outgo_a, from_in, channel, i, j, 1, inner).wait_recv()

                if_mine(i, j, wait)
                finish_block(
                    channel, i, j, i == 1,
                    lambda: part[channel, slot]
                    + from_out[channel, slot].astype(F32)
                    + from_in[channel, slot].astype(F32),
                )

    def collect(channel):
        for block in range(CHIPS):

            @pl.when(chip != block)
            def _():
                swap(channel, block, pl.ds(1 - core, 1)).wait_recv()
                put(channel, block, 1 - core, arrived[channel, 1 - core, :, block * BLK : (block + 1) * BLK])

            @pl.when(jnp.logical_and(chip == block, core != block % 2))
            def _():
                swap(channel, block, pl.ds(0, 2)).wait_recv()
                for plane in range(2):
                    put(channel, block, plane, arrived[channel, plane, :, block * BLK : (block + 1) * BLK])

    def vis_copy(channel):
        return pltpu.make_async_copy(rows_out.at[:, channel], vis_out.at[:, channel], out_sem.at[2 + channel])

    gather(0)
    spec_copy(0).start()
    for copy in pair_copies(0, pl.ds(0, NIN)):
        copy.wait_recv()
    products(0)
    gather(1)
    spec_copy(1).start()
    for copy in pair_copies(1, pl.ds(0, NIN)):
        copy.wait_recv()
    products(1)
    finish(0)
    collect(0)
    vis_copy(0).start()
    finish(1)
    collect(1)
    vis_copy(1).start()

    @pl.when(ta < 2 * CHIPS - 1)
    def _():
        halo.wait_send()

    for channel in range(2):

        def drain(step, carry, channel=channel):
            to_owner(channel, (col + step) % COLS, pl.ds(0, QF)).wait_send()
            return carry

        lax.fori_loop(1, COLS, drain, 0)
        for copy in pair_copies(channel, pl.ds(0, NIN)):
            copy.wait_send()

        @pl.when(is_end)
        def _():
            for i, j in ORDER:
                if j >= 1:
                    if_mine(i, j, lambda: stream(outgo_a, from_out, channel, i, j, 0, inner).wait_send())

        @pl.when(is_middle)
        def _():
            for i, j in inward:
                if_mine(i, j, lambda: stream(outgo_a, from_in, channel, i, j, 1, inner).wait_send())
            for i, j in outward:
                if_mine(i, j, lambda: stream(outgo_b, from_in, channel, i, j, 2, outer).wait_send())

        for block in range(CHIPS):

            @pl.when(chip != block)
            def _():
                swap(channel, block, pl.ds(core, 1)).wait_send()

            @pl.when(jnp.logical_and(chip == block, core == block % 2))
            def _():
                swap(channel, block, pl.ds(0, 2)).wait_send()

        spec_copy(channel).wait()
        vis_copy(channel).wait()


def body(voltages, taps_filter):
    blocks = (2, len(ORDER), BLK, BLK)
    spectra, visib = pl.pallas_call(
        kernel,
        out_shape=(
            jax.ShapeDtypeStruct((2, 2 * FRAMES, NIN), BF16),
            jax.ShapeDtypeStruct((128, 2, 2, NIN), F32),
        ),
        in_specs=[
            pl.BlockSpec(memory_space=pl.ANY),
            pl.BlockSpec(memory_space=pltpu.VMEM),
            pl.BlockSpec(memory_space=pltpu.VMEM),
        ],
        out_specs=(pl.BlockSpec(memory_space=pl.ANY), pl.BlockSpec(memory_space=pl.ANY)),
        scratch_shapes=[
            pltpu.VMEM((FRAMES + TAPS, LOCAL, FR), BF16),
            pltpu.VMEM((JC, FR, FR), BF16),
            pltpu.VMEM((JC * FR, FR), F32),
            pltpu.VMEM((FR, QF, FR), BF16),
            pltpu.VMEM((COLS, 4, QF, FR), BF16),
            pltpu.VMEM((2, 2 * FRAMES, NIN), BF16),
            pltpu.VMEM((2, NIN, 4 * FRAMES), BF16),
            pltpu.VMEM((2, 4 * FRAMES, NIN), BF16),
            pltpu.VMEM((2, 2 * FRAMES, NIN), BF16),
            pltpu.VMEM(blocks, F32),
            pltpu.VMEM(blocks, BF16),
            pltpu.VMEM(blocks, BF16),
            pltpu.VMEM(blocks, BF16),
            pltpu.VMEM(blocks, BF16),
            pltpu.VMEM((2, BLK, BLK), F32),
            pltpu.VMEM((2, 2, 128, NIN), F32),
            pltpu.VMEM((2, 2, 128, NIN), F32),
            pltpu.VMEM((128, 2, 2, NIN), F32),
            pltpu.SemaphoreType.DMA((1,)),
            pltpu.SemaphoreType.DMA((2,)),
            pltpu.SemaphoreType.DMA((2, COLS)),
            pltpu.SemaphoreType.DMA((2, COLS)),
            pltpu.SemaphoreType.DMA((1,)),
            pltpu.SemaphoreType.DMA((2, 2)),
            pltpu.SemaphoreType.DMA((2, 2)),
            pltpu.SemaphoreType.DMA((2, 3, len(ORDER))),
            pltpu.SemaphoreType.DMA((2, 3, len(ORDER))),
            pltpu.SemaphoreType.DMA((2, CHIPS)),
            pltpu.SemaphoreType.DMA((2, CHIPS)),
            pltpu.SemaphoreType.DMA((4,)),
        ],
        compiler_params=pltpu.CompilerParams(
            collective_id=0, has_side_effects=True, vmem_limit_bytes=60 * 2**20
        ),
        name="correlator",
    )(voltages, taps_filter, make_table_rows())
    return spectra.reshape(2, 2, FRAMES, NIN), visib


def solution(mesh):
    return jax.shard_map(
        body,
        mesh=mesh,
        in_specs=(P("ta", "col", None), P()),
        out_specs=(P("col", None, "ta", None), P("ta", "col", None, None)),
        check_vma=False,
    )
```

```python
import jax
import jax.numpy as jnp
import numpy as np
from jax import lax
from jax.experimental import pallas as pl
from jax.experimental.pallas import tpu as pltpu
from jax.sharding import PartitionSpec as P

MESH = pl.DeviceIdType.MESH
F32 = jnp.float32
BF16 = jnp.bfloat16

TAPS = 16
FR = 128
FRAMES = 256
LOCAL = 32
COLS = 32
NIN = 1024
CHIPS = 4
BLK = NIN // CHIPS
QF = FRAMES // 4
JC = 16
NJC = QF // JC
GROUPS = COLS // 4

ORDER = [(i, j) for j in range(CHIPS - 1, -1, -1) for i in range(j + 1)]


def make_table_rows():
    row = lax.broadcasted_iota(jnp.int32, (FR, FR), 0)
    sample = lax.broadcasted_iota(jnp.int32, (FR, FR), 1)
    phase = ((row // 2) * sample + (row % 2) * (FR // 4)) % FR
    return jnp.cos(phase.astype(F32) * (2.0 * np.pi / FR)).astype(BF16)


def kernel(
    volt, taps, spec_out, vis_out,
    table, padded, filt, wide, sendbuf, recvbuf, spectra, across, right, for_sibling, part, outgo_a, outgo_b, from_out, from_in, work, stage, arrived, rows_out,
    load_sem, halo_sem, a2a_send, a2a_recv, own_sem, pair_send, pair_recv, line_send, line_recv, half_send, half_recv, out_sem,
):
    ta = lax.axis_index("ta")
    col = lax.axis_index("col")
    chip = ta // 2
    core = ta % 2
    mirror = chip // 2
    middle = chip * (1 - mirror) + (3 - chip) * mirror
    inner = {"ta": (chip + 1 - 2 * mirror) * 2 + core, "col": col}
    outer = {"ta": (chip - 1 + 2 * mirror) * 2 + core, "col": col}
    sibling = {"ta": chip * 2 + 1 - core, "col": col}
    before = {"ta": ta - 1, "col": col}
    after = {"ta": ta + 1, "col": col}
    is_end = middle == 0
    is_middle = middle == 1
    cross_after = jnp.logical_and(core == 1, chip < CHIPS - 1)
    cross_before = jnp.logical_and(core == 0, chip > 0)

    def loads(half):
        return [
            pltpu.make_async_copy(
                volt.at[pl.ds(b * QF + half * (QF // 2), QF // 2)],
                padded.at[pl.ds(TAPS + b * QF + half * (QF // 2), QF // 2)],
                load_sem.at[half, b],
            )
            for b in range(4)
        ]

    for half in range(2):
        for load in loads(half):
            load.start()

    barrier = pltpu.get_barrier_semaphore()

    def greet(device):
        pl.semaphore_signal(barrier, inc=1, device_id=device, device_id_type=MESH)

    def greet_col(step, carry):
        greet({"ta": ta, "col": (col + step) % COLS})
        return carry

    lax.fori_loop(1, COLS, greet_col, 0)
    greet(sibling)
    greet(inner)

    @pl.when(is_middle)
    def _():
        greet(outer)

    @pl.when(cross_after)
    def _():
        greet(after)

    @pl.when(cross_before)
    def _():
        greet(before)

    @pl.when(ta == 0)
    def _():
        padded[0:TAPS] = jnp.zeros((TAPS, LOCAL, FR), BF16)

    table[...] = make_table_rows()
    for load in loads(0):
        load.wait()

    def front(chunk):
        def filter_part(step, carry):
            group = step // 2
            rows = pl.ds(pl.multiple_of((step % 2) * 16, 16), 16)
            out_rows = pl.ds(pl.multiple_of(group * LOCAL + (step % 2) * 16, 16), 16)
            weights = [taps[t : t + 1, :] for t in range(TAPS)]
            for part_of in range(JC // 8):
                base = group * QF + chunk * JC + part_of * 8 + 1
                held = [padded[base + i, rows, :].astype(F32) for i in range(TAPS + 7)]
                for o in range(8):
                    total = weights[0] * held[o]
                    for t in range(1, TAPS):
                        total = total + weights[t] * held[o + t]
                    filt[part_of * 8 + o, out_rows, :] = total.astype(BF16)
            return carry

        lax.fori_loop(0, 8, filter_part, 0)
        for j in range(JC):
            wide[pl.ds(j, FR, stride=JC), :] = lax.dot_general(
                table[...], filt[j], (((1,), (1,)), ((), ())), preferred_element_type=F32
            )
        sendbuf[:, pl.ds(chunk * JC, JC), :] = wide[...].reshape(FR, JC, FR).astype(BF16)

    def to_owner(channel, peer, rows):
        return pltpu.make_async_remote_copy(
            src_ref=sendbuf.at[pl.ds(peer * 4 + 2 * channel, 2), rows],
            dst_ref=recvbuf.at[col, pl.ds(2 * channel, 2), rows],
            send_sem=a2a_send.at[channel, peer],
            recv_sem=a2a_recv.at[channel, col],
            device_id={"ta": ta, "col": peer},
            device_id_type=MESH,
        )

    def send_chunk(channel, rows):
        def send_one(step, carry):
            to_owner(channel, (col + step) % COLS, rows).start()
            return carry

        lax.fori_loop(1, COLS, send_one, 0)

    halo = pltpu.make_async_remote_copy(
        src_ref=padded.at[pl.ds(FRAMES, TAPS)],
        dst_ref=padded.at[pl.ds(0, TAPS)],
        send_sem=halo_sem.at[0],
        recv_sem=halo_sem.at[1],
        device_id=after,
        device_id_type=MESH,
    )

    front(1)
    for load in loads(1):
        load.wait()
    pl.semaphore_wait(
        barrier,
        COLS + 1 + middle + cross_after.astype(jnp.int32) + cross_before.astype(jnp.int32),
    )

    @pl.when(ta < 2 * CHIPS - 1)
    def _():
        halo.start()

    send_chunk(0, pl.ds(1 * JC, JC))
    front(2)
    send_chunk(0, pl.ds(2 * JC, JC))
    front(3)
    send_chunk(0, pl.ds(3 * JC, JC))

    @pl.when(ta > 0)
    def _():
        halo.wait_recv()

    front(0)
    send_chunk(0, pl.ds(0 * JC, JC))
    send_chunk(1, pl.ds(0, QF))
    own = pltpu.make_async_copy(sendbuf.at[pl.ds(col * 4, 4)], recvbuf.at[col], own_sem.at[0])
    own.start()

    def pair_copies(channel, lanes):
        own_k, sibling_k = pl.ds(0, 2 * FRAMES), pl.ds(2 * FRAMES, 2 * FRAMES)
        ways = [
            (across.at[channel, lanes, own_k], across.at[channel, lanes, sibling_k]),
            (for_sibling.at[channel, :, lanes], right.at[channel, sibling_k, lanes]),
        ]
        return [
            pltpu.make_async_remote_copy(
                src_ref=src,
                dst_ref=dst,
                send_sem=pair_send.at[channel, way],
                recv_sem=pair_recv.at[channel, way],
                device_id=sibling,
                device_id_type=MESH,
            )
            for way, (src, dst) in enumerate(ways)
        ]

    def gather(channel):
        def regroup_one(g, carry):
            lanes = pl.ds(pl.multiple_of(g * 128, 128), 128)
            for i in range(4):
                source = g * 4 + i

                @pl.when(source != col)
                def _():
                    pltpu.make_async_remote_copy(
                        src_ref=recvbuf.at[source, pl.ds(2 * channel, 2)],
                        dst_ref=recvbuf.at[source, pl.ds(2 * channel, 2)],
                        send_sem=a2a_send.at[channel, source],
                        recv_sem=a2a_recv.at[channel, source],
                        device_id={"ta": ta, "col": source},
                        device_id_type=MESH,
                    ).wait_recv()

            for r in range(2):
                held = [recvbuf[g * 4 + i, 2 * channel + r] for i in range(4)]
                value = jnp.concatenate(
                    [
                        jnp.concatenate([h[:, b * LOCAL : (b + 1) * LOCAL] for h in held], axis=1)
                        for b in range(4)
                    ],
                    axis=0,
                )
                here, there = pl.ds(r * FRAMES, FRAMES), pl.ds((1 - r) * FRAMES, FRAMES)
                spectra[channel, here, lanes] = value
                across[channel, lanes, here] = value.T

                @pl.when(core == 0)
                def _():
                    right[channel, here, lanes] = value
                    for_sibling[channel, there, lanes] = value if r == 1 else -value

                @pl.when(core == 1)
                def _():
                    right[channel, there, lanes] = value if r == 1 else -value
                    for_sibling[channel, here, lanes] = value

            for copy in pair_copies(channel, lanes):
                copy.start()
            return carry

        lax.fori_loop(0, GROUPS, regroup_one, 0)

    def spec_copy(channel):
        return pltpu.make_async_copy(spectra.at[channel], spec_out.at[channel], out_sem.at[channel])

    def actual(i, j):
        return i + mirror * (3 - i - j), j + mirror * (3 - i - j)

    def slot_of(i, j):
        rows, columns = actual(i, j)
        return columns * (columns + 1) // 2 + rows

    def lanes_of(block):
        return pl.ds(pl.multiple_of(block * BLK, BLK), BLK)

    def mine(channel, i, j):
        return None if i != j else core == (i + mirror + channel) % 2

    def if_mine(channel, i, j, run):
        if i == j:
            pl.when(mine(channel, i, j))(run)
        else:
            run()

    def stream(buffer, landing, channel, i, j, way, device):
        slot = slot_of(i, j)
        return pltpu.make_async_remote_copy(
            src_ref=buffer.at[channel, slot],
            dst_ref=landing.at[channel, slot],
            send_sem=line_send.at[channel, way, slot],
            recv_sem=line_recv.at[channel, way, slot],
            device_id=device,
            device_id_type=MESH,
        )


    row_id = lax.broadcasted_iota(jnp.int32, (BLK, BLK), 0)
    col_id = lax.broadcasted_iota(jnp.int32, (BLK, BLK), 1)
    inward = [(i, j) for i, j in ORDER if j >= 2]
    outward = [(0, j) for j in range(CHIPS - 1, -1, -1)]
    forwards = {
        (0, 3): [("in", 0, 3)],
        (1, 3): [("in", 1, 3)],
        (2, 3): [("in", 2, 3)],
        (3, 3): [("in", 3, 3), ("out", 0, 3)],
        (0, 2): [("out", 0, 2)],
        (0, 1): [("out", 0, 1)],
        (0, 0): [("out", 0, 0), ("in", 0, 2), ("in", 1, 2), ("in", 2, 2)],
    }

    def product(channel, i, j):
        rows, columns = actual(i, j)
        slot = slot_of(i, j)
        lhs = across[channel, lanes_of(rows), :]
        value = jnp.dot(lhs, right[channel, :, lanes_of(columns)], preferred_element_type=F32)
        if i == j:
            other = jnp.zeros((BLK, BLK), F32)
            for k in range(4):
                term = jnp.dot(
                    lhs[:, k * FRAMES : (k + 1) * FRAMES],
                    right[channel, (k ^ 1) * FRAMES : ((k ^ 1) + 1) * FRAMES, lanes_of(columns)],
                    preferred_element_type=F32,
                )
                other = other + term if k % 2 == 0 else other - term
            real = jnp.where(core == 0, value, -other)
            imag = jnp.where(core == 0, other, value)
            value = jnp.where(row_id <= col_id, real, imag)
        part[channel, slot] = value
        if j >= 1:

            @pl.when(is_end)
            def _():
                outgo_a[channel, slot] = value.astype(BF16)
                stream(outgo_a, from_out, channel, i, j, 0, inner).start()

    def to_inner(channel, i, j):
        slot = slot_of(i, j)
        stream(outgo_a, from_out, channel, i, j, 0, outer).wait_recv()
        outgo_a[channel, slot] = (part[channel, slot] + from_out[channel, slot].astype(F32)).astype(BF16)
        stream(outgo_a, from_in, channel, i, j, 1, inner).start()

    def to_outer(channel, i, j):
        slot = slot_of(i, j)
        stream(outgo_b, from_in, channel, i, j, 1, inner).wait_recv()
        outgo_b[channel, slot] = (part[channel, slot] + from_in[channel, slot].astype(F32)).astype(BF16)
        stream(outgo_b, from_in, channel, i, j, 2, outer).start()

    def products(channel):
        for i, j in ORDER:
            if_mine(channel, i, j, lambda: product(channel, i, j))

            if (i, j) in forwards:

                @pl.when(is_middle)
                def _():
                    for way, k, l in forwards[i, j]:
                        if_mine(channel, k, l, lambda: (to_inner if way == "in" else to_outer)(channel, k, l))

    scale = 1.0 / (FRAMES * 2 * CHIPS)

    def swap(channel, block, planes):
        return pltpu.make_async_remote_copy(
            src_ref=stage.at[channel, planes, :, lanes_of(block)],
            dst_ref=arrived.at[channel, planes, :, lanes_of(block)],
            send_sem=half_send.at[channel, block],
            recv_sem=half_recv.at[channel, block],
            device_id=sibling,
            device_id_type=MESH,
        )

    def put(channel, block, plane, value):
        rows_out[:, channel, plane, lanes_of(block)] = value

    own_rows = pl.ds(pl.multiple_of(core * 128, 128), 128)
    other_rows = pl.ds(pl.multiple_of((1 - core) * 128, 128), 128)

    def finish_block(channel, i, j, own_is_row, total):
        rows, columns = actual(i, j)
        if i == j:

            @pl.when(mine(channel, i, j))
            def _():
                packed = total() * scale
                flipped = packed.T
                work[0] = jnp.where(row_id <= col_id, packed, flipped)
                work[1] = jnp.where(row_id > col_id, packed, jnp.where(row_id == col_id, 0.0, -flipped))
                for plane in range(2):
                    stage[channel, plane, :, lanes_of(rows)] = work[plane, other_rows, :]
                swap(channel, rows, pl.ds(0, 2)).start()
                for plane in range(2):
                    put(channel, rows, plane, work[plane, own_rows, :])

        else:
            straight = mirror == (0 if own_is_row else 1)
            block = columns * straight.astype(jnp.int32) + rows * (1 - straight.astype(jnp.int32))

            @pl.when(straight)
            def _():
                work[0] = total() * scale

            @pl.when(jnp.logical_not(straight))
            def _():
                work[0] = total().T * (scale * (1 - 2 * core).astype(F32))

            stage[channel, core, :, lanes_of(block)] = work[0, other_rows, :]
            swap(channel, block, pl.ds(core, 1)).start()
            put(channel, block, core, work[0, own_rows, :])

    def finish(channel):
        @pl.when(is_end)
        def _():
            for i, j in outward:
                slot = slot_of(i, j)

                def wait(i=i, j=j):
                    stream(outgo_b, from_in, channel, i, j, 2, inner).wait_recv()

                if_mine(channel, i, j, wait)
                finish_block(
                    channel, i, j, True, lambda: part[channel, slot] + from_in[channel, slot].astype(F32)
                )

        @pl.when(is_middle)
        def _():
            for i, j in [(1, 3), (1, 2), (0, 1), (1, 1)]:
                slot = slot_of(i, j)

                def wait(i=i, j=j):
                    if j == 1:
                        stream(outgo_a, from_out, channel, i, j, 0, outer).wait_recv()
                    if i == 1:
                        stream(outgo_a, from_in, channel, i, j, 1, inner).wait_recv()

                if_mine(channel, i, j, wait)
                finish_block(
                    channel, i, j, i == 1,
                    lambda: part[channel, slot]
                    + from_out[channel, slot].astype(F32)
                    + from_in[channel, slot].astype(F32),
                )

    def block_copy(channel, block):
        lanes = lanes_of(block)
        return pltpu.make_async_copy(
            rows_out.at[:, channel, :, lanes], vis_out.at[:, channel, :, lanes], out_sem.at[2 + channel]
        )

    def collect(channel):
        for place in (3, 2, 1 - middle, middle):
            block = place + mirror * (3 - 2 * place)
            if place is not middle:
                swap(channel, block, pl.ds(1 - core, 1)).wait_recv()
                put(channel, block, 1 - core, arrived[channel, 1 - core, :, lanes_of(block)])
            else:

                @pl.when(core != (block + channel) % 2)
                def _():
                    swap(channel, block, pl.ds(0, 2)).wait_recv()
                    for plane in range(2):
                        put(channel, block, plane, arrived[channel, plane, :, lanes_of(block)])

            block_copy(channel, block).start()

    def vis_copy(channel):
        return pltpu.make_async_copy(rows_out.at[:, channel], vis_out.at[:, channel], out_sem.at[2 + channel])

    own.wait()
    gather(0)
    spec_copy(0).start()
    for copy in pair_copies(0, pl.ds(0, NIN)):
        copy.wait_recv()
    products(0)
    gather(1)
    spec_copy(1).start()
    for copy in pair_copies(1, pl.ds(0, NIN)):
        copy.wait_recv()
    products(1)
    finish(0)
    collect(0)
    finish(1)
    collect(1)

    @pl.when(ta < 2 * CHIPS - 1)
    def _():
        halo.wait_send()

    for channel in range(2):

        def drain(step, carry, channel=channel):
            to_owner(channel, (col + step) % COLS, pl.ds(0, QF)).wait_send()
            return carry

        lax.fori_loop(1, COLS, drain, 0)
        for copy in pair_copies(channel, pl.ds(0, NIN)):
            copy.wait_send()

        @pl.when(is_end)
        def _():
            for i, j in ORDER:
                if j >= 1:
                    if_mine(channel, i, j, lambda: stream(outgo_a, from_out, channel, i, j, 0, inner).wait_send())

        @pl.when(is_middle)
        def _():
            for i, j in inward:
                if_mine(channel, i, j, lambda: stream(outgo_a, from_in, channel, i, j, 1, inner).wait_send())
            for i, j in outward:
                if_mine(channel, i, j, lambda: stream(outgo_b, from_in, channel, i, j, 2, outer).wait_send())

        for block in range(CHIPS):

            @pl.when(chip != block)
            def _():
                swap(channel, block, pl.ds(core, 1)).wait_send()

            @pl.when(jnp.logical_and(chip == block, core == (block + channel) % 2))
            def _():
                swap(channel, block, pl.ds(0, 2)).wait_send()

        spec_copy(channel).wait()
        vis_copy(channel).wait()


def body(voltages, taps_filter):
    blocks = (2, len(ORDER), BLK, BLK)
    spectra, visib = pl.pallas_call(
        kernel,
        out_shape=(
            jax.ShapeDtypeStruct((2, 2 * FRAMES, NIN), BF16),
            jax.ShapeDtypeStruct((128, 2, 2, NIN), F32),
        ),
        in_specs=[
            pl.BlockSpec(memory_space=pl.ANY),
            pl.BlockSpec(memory_space=pltpu.VMEM),
        ],
        out_specs=(pl.BlockSpec(memory_space=pl.ANY), pl.BlockSpec(memory_space=pl.ANY)),
        scratch_shapes=[
            pltpu.VMEM((FR, FR), BF16),
            pltpu.VMEM((FRAMES + TAPS, LOCAL, FR), BF16),
            pltpu.VMEM((JC, FR, FR), BF16),
            pltpu.VMEM((JC * FR, FR), F32),
            pltpu.VMEM((FR, QF, FR), BF16),
            pltpu.VMEM((COLS, 4, QF, FR), BF16),
            pltpu.VMEM((2, 2 * FRAMES, NIN), BF16),
            pltpu.VMEM((2, NIN, 4 * FRAMES), BF16),
            pltpu.VMEM((2, 4 * FRAMES, NIN), BF16),
            pltpu.VMEM((2, 2 * FRAMES, NIN), BF16),
            pltpu.VMEM(blocks, F32),
            pltpu.VMEM(blocks, BF16),
            pltpu.VMEM(blocks, BF16),
            pltpu.VMEM(blocks, BF16),
            pltpu.VMEM(blocks, BF16),
            pltpu.VMEM((2, BLK, BLK), F32),
            pltpu.VMEM((2, 2, 128, NIN), F32),
            pltpu.VMEM((2, 2, 128, NIN), F32),
            pltpu.VMEM((128, 2, 2, NIN), F32),
            pltpu.SemaphoreType.DMA((2, 4)),
            pltpu.SemaphoreType.DMA((2,)),
            pltpu.SemaphoreType.DMA((2, COLS)),
            pltpu.SemaphoreType.DMA((2, COLS)),
            pltpu.SemaphoreType.DMA((1,)),
            pltpu.SemaphoreType.DMA((2, 2)),
            pltpu.SemaphoreType.DMA((2, 2)),
            pltpu.SemaphoreType.DMA((2, 3, len(ORDER))),
            pltpu.SemaphoreType.DMA((2, 3, len(ORDER))),
            pltpu.SemaphoreType.DMA((2, CHIPS)),
            pltpu.SemaphoreType.DMA((2, CHIPS)),
            pltpu.SemaphoreType.DMA((4,)),
        ],
        compiler_params=pltpu.CompilerParams(
            collective_id=0, has_side_effects=True, vmem_limit_bytes=48 * 2**20
        ),
        name="correlator",
    )(voltages, taps_filter)
    return spectra.reshape(2, 2, FRAMES, NIN), visib


def solution(mesh):
    return jax.shard_map(
        body,
        mesh=mesh,
        in_specs=(P("ta", "col", None), P()),
        out_specs=(P("col", None, "ta", None), P("ta", "col", None, None)),
        check_vma=False,
    )
```

```python
import jax
import jax.numpy as jnp
import numpy as np
from jax import lax
from jax.experimental import pallas as pl
from jax.experimental.pallas import tpu as pltpu
from jax.sharding import PartitionSpec as P

MESH = pl.DeviceIdType.MESH
F32 = jnp.float32
BF16 = jnp.bfloat16

TAPS = 16
FR = 128
FRAMES = 256
LOCAL = 32
COLS = 32
NIN = 1024
CHIPS = 4
BLK = NIN // CHIPS
QF = FRAMES // 4
JC = 16
NJC = QF // JC
GROUPS = COLS // 4

ORDER = [(0, 3), (1, 3), (2, 3), (3, 3), (0, 2), (1, 2), (2, 2), (1, 1), (0, 1), (0, 0)]


def make_table_rows():
    row = lax.broadcasted_iota(jnp.int32, (FR, FR), 0)
    sample = lax.broadcasted_iota(jnp.int32, (FR, FR), 1)
    phase = ((row // 2) * sample + (row % 2) * (FR // 4)) % FR
    return jnp.cos(phase.astype(F32) * (2.0 * np.pi / FR)).astype(BF16)


def kernel(
    volt, taps, spec_out, vis_out,
    table, padded, filt, wide, sendbuf, recvbuf, spectra, across, right, for_sibling, part, outgo_a, outgo_b, from_out, from_in, work, stage, arrived, rows_out,
    load_sem, halo_sem, a2a_send, a2a_recv, own_sem, pair_send, pair_recv, line_send, line_recv, half_send, half_recv, out_sem,
):
    ta = lax.axis_index("ta")
    col = lax.axis_index("col")
    chip = ta // 2
    core = ta % 2
    mirror = chip // 2
    middle = chip * (1 - mirror) + (3 - chip) * mirror
    inner = {"ta": (chip + 1 - 2 * mirror) * 2 + core, "col": col}
    outer = {"ta": (chip - 1 + 2 * mirror) * 2 + core, "col": col}
    sibling = {"ta": chip * 2 + 1 - core, "col": col}
    before = {"ta": ta - 1, "col": col}
    after = {"ta": ta + 1, "col": col}
    is_end = middle == 0
    is_middle = middle == 1
    cross_after = jnp.logical_and(core == 1, chip < CHIPS - 1)
    cross_before = jnp.logical_and(core == 0, chip > 0)

    def loads(half):
        return [
            pltpu.make_async_copy(
                volt.at[pl.ds(b * QF + half * (QF // 2), QF // 2)],
                padded.at[pl.ds(TAPS + b * QF + half * (QF // 2), QF // 2)],
                load_sem.at[half, b],
            )
            for b in range(4)
        ]

    for half in range(2):
        for load in loads(half):
            load.start()

    barrier = pltpu.get_barrier_semaphore()

    def greet(device):
        pl.semaphore_signal(barrier, inc=1, device_id=device, device_id_type=MESH)

    def greet_col(step, carry):
        greet({"ta": ta, "col": (col + step) % COLS})
        return carry

    lax.fori_loop(1, COLS, greet_col, 0)
    greet(sibling)
    greet(inner)

    @pl.when(is_middle)
    def _():
        greet(outer)

    @pl.when(cross_after)
    def _():
        greet(after)

    @pl.when(cross_before)
    def _():
        greet(before)

    @pl.when(ta == 0)
    def _():
        padded[0:TAPS] = jnp.zeros((TAPS, LOCAL, FR), BF16)

    table[...] = make_table_rows()
    for load in loads(0):
        load.wait()

    def front(chunk):
        def filter_part(step, carry):
            group = step // 2
            rows = pl.ds(pl.multiple_of((step % 2) * 16, 16), 16)
            out_rows = pl.ds(pl.multiple_of(group * LOCAL + (step % 2) * 16, 16), 16)
            weights = [taps[t : t + 1, :] for t in range(TAPS)]
            for part_of in range(JC // 8):
                base = group * QF + chunk * JC + part_of * 8 + 1
                held = [padded[base + i, rows, :].astype(F32) for i in range(TAPS + 7)]
                for o in range(8):
                    total = weights[0] * held[o]
                    for t in range(1, TAPS):
                        total = total + weights[t] * held[o + t]
                    filt[part_of * 8 + o, out_rows, :] = total.astype(BF16)
            return carry

        lax.fori_loop(0, 8, filter_part, 0)
        for j in range(JC):
            wide[pl.ds(j, FR, stride=JC), :] = lax.dot_general(
                table[...], filt[j], (((1,), (1,)), ((), ())), preferred_element_type=F32
            )
        sendbuf[:, pl.ds(chunk * JC, JC), :] = wide[...].reshape(FR, JC, FR).astype(BF16)

    def to_owner(channel, peer, rows):
        return pltpu.make_async_remote_copy(
            src_ref=sendbuf.at[pl.ds(peer * 4 + 2 * channel, 2), rows],
            dst_ref=recvbuf.at[col, pl.ds(2 * channel, 2), rows],
            send_sem=a2a_send.at[channel, peer],
            recv_sem=a2a_recv.at[channel, col],
            device_id={"ta": ta, "col": peer},
            device_id_type=MESH,
        )

    def send_chunk(channel, rows):
        def send_one(step, carry):
            to_owner(channel, (col + step) % COLS, rows).start()
            return carry

        lax.fori_loop(1, COLS, send_one, 0)

    halo = pltpu.make_async_remote_copy(
        src_ref=padded.at[pl.ds(FRAMES, TAPS)],
        dst_ref=padded.at[pl.ds(0, TAPS)],
        send_sem=halo_sem.at[0],
        recv_sem=halo_sem.at[1],
        device_id=after,
        device_id_type=MESH,
    )

    front(1)
    for load in loads(1):
        load.wait()
    pl.semaphore_wait(
        barrier,
        COLS + 1 + middle + cross_after.astype(jnp.int32) + cross_before.astype(jnp.int32),
    )

    @pl.when(ta < 2 * CHIPS - 1)
    def _():
        halo.start()

    send_chunk(0, pl.ds(1 * JC, JC))
    front(2)
    send_chunk(0, pl.ds(2 * JC, JC))
    front(3)
    send_chunk(0, pl.ds(3 * JC, JC))

    @pl.when(ta > 0)
    def _():
        halo.wait_recv()

    front(0)
    send_chunk(0, pl.ds(0 * JC, JC))
    send_chunk(1, pl.ds(0, QF))
    own = pltpu.make_async_copy(sendbuf.at[pl.ds(col * 4, 4)], recvbuf.at[col], own_sem.at[0])
    own.start()

    def pair_copies(channel, lanes):
        own_k, sibling_k = pl.ds(0, 2 * FRAMES), pl.ds(2 * FRAMES, 2 * FRAMES)
        ways = [
            (across.at[channel, lanes, own_k], across.at[channel, lanes, sibling_k]),
            (for_sibling.at[channel, :, lanes], right.at[channel, sibling_k, lanes]),
        ]
        return [
            pltpu.make_async_remote_copy(
                src_ref=src,
                dst_ref=dst,
                send_sem=pair_send.at[channel, way],
                recv_sem=pair_recv.at[channel, way],
                device_id=sibling,
                device_id_type=MESH,
            )
            for way, (src, dst) in enumerate(ways)
        ]

    def gather(channel):
        def regroup_one(g, carry):
            lanes = pl.ds(pl.multiple_of(g * 128, 128), 128)
            for i in range(4):
                source = g * 4 + i

                @pl.when(source != col)
                def _():
                    pltpu.make_async_remote_copy(
                        src_ref=recvbuf.at[source, pl.ds(2 * channel, 2)],
                        dst_ref=recvbuf.at[source, pl.ds(2 * channel, 2)],
                        send_sem=a2a_send.at[channel, source],
                        recv_sem=a2a_recv.at[channel, source],
                        device_id={"ta": ta, "col": source},
                        device_id_type=MESH,
                    ).wait_recv()

            for r in range(2):
                held = [recvbuf[g * 4 + i, 2 * channel + r] for i in range(4)]
                value = jnp.concatenate(
                    [
                        jnp.concatenate([h[:, b * LOCAL : (b + 1) * LOCAL] for h in held], axis=1)
                        for b in range(4)
                    ],
                    axis=0,
                )
                here, there = pl.ds(r * FRAMES, FRAMES), pl.ds((1 - r) * FRAMES, FRAMES)
                spectra[channel, here, lanes] = value
                across[channel, lanes, here] = value.T

                @pl.when(core == 0)
                def _():
                    right[channel, here, lanes] = value
                    for_sibling[channel, there, lanes] = value if r == 1 else -value

                @pl.when(core == 1)
                def _():
                    right[channel, there, lanes] = value if r == 1 else -value
                    for_sibling[channel, here, lanes] = value

            for copy in pair_copies(channel, lanes):
                copy.start()
            return carry

        lax.fori_loop(0, GROUPS, regroup_one, 0)

    def spec_copy(channel):
        return pltpu.make_async_copy(spectra.at[channel], spec_out.at[channel], out_sem.at[channel])

    def actual(i, j):
        return i + mirror * (3 - i - j), j + mirror * (3 - i - j)

    def slot_of(i, j):
        rows, columns = actual(i, j)
        return columns * (columns + 1) // 2 + rows

    def lanes_of(block):
        return pl.ds(pl.multiple_of(block * BLK, BLK), BLK)

    def mine(channel, i, j):
        return None if i != j else core == (i + mirror + channel) % 2

    def if_mine(channel, i, j, run):
        if i == j:
            pl.when(mine(channel, i, j))(run)
        else:
            run()

    def stream(buffer, landing, channel, i, j, way, device):
        slot = slot_of(i, j)
        return pltpu.make_async_remote_copy(
            src_ref=buffer.at[channel, slot],
            dst_ref=landing.at[channel, slot],
            send_sem=line_send.at[channel, way, slot],
            recv_sem=line_recv.at[channel, way, slot],
            device_id=device,
            device_id_type=MESH,
        )


    row_id = lax.broadcasted_iota(jnp.int32, (BLK, BLK), 0)
    col_id = lax.broadcasted_iota(jnp.int32, (BLK, BLK), 1)
    inward = [(i, j) for i, j in ORDER if j >= 2]
    outward = [(0, j) for j in range(CHIPS - 1, -1, -1)]
    forwards = {
        (0, 3): [("in", 0, 3)],
        (1, 3): [("in", 1, 3)],
        (2, 3): [("in", 2, 3)],
        (3, 3): [("in", 3, 3), ("out", 0, 3)],
        (0, 2): [("out", 0, 2)],
        (0, 1): [("out", 0, 1)],
        (0, 0): [("out", 0, 0), ("in", 0, 2), ("in", 1, 2), ("in", 2, 2)],
    }

    def product(channel, i, j):
        rows, columns = actual(i, j)
        slot = slot_of(i, j)
        lhs = across[channel, lanes_of(rows), :]
        value = jnp.dot(lhs, right[channel, :, lanes_of(columns)], preferred_element_type=F32)
        if i == j:
            other = jnp.zeros((BLK, BLK), F32)
            for k in range(4):
                term = jnp.dot(
                    lhs[:, k * FRAMES : (k + 1) * FRAMES],
                    right[channel, (k ^ 1) * FRAMES : ((k ^ 1) + 1) * FRAMES, lanes_of(columns)],
                    preferred_element_type=F32,
                )
                other = other + term if k % 2 == 0 else other - term
            real = jnp.where(core == 0, value, -other)
            imag = jnp.where(core == 0, other, value)
            value = jnp.where(row_id <= col_id, real, imag)
        part[channel, slot] = value
        if j >= 1:

            @pl.when(is_end)
            def _():
                outgo_a[channel, slot] = value.astype(BF16)
                if j >= 2 or channel == 1:
                    stream(outgo_a, from_out, channel, i, j, 0, inner).start()

    def to_inner(channel, i, j):
        slot = slot_of(i, j)
        stream(outgo_a, from_out, channel, i, j, 0, outer).wait_recv()
        outgo_a[channel, slot] = (part[channel, slot] + from_out[channel, slot].astype(F32)).astype(BF16)
        stream(outgo_a, from_in, channel, i, j, 1, inner).start()

    def to_outer(channel, i, j):
        slot = slot_of(i, j)
        stream(outgo_b, from_in, channel, i, j, 1, inner).wait_recv()
        outgo_b[channel, slot] = (part[channel, slot] + from_in[channel, slot].astype(F32)).astype(BF16)
        stream(outgo_b, from_in, channel, i, j, 2, outer).start()

    def products(channel):
        for i, j in ORDER:
            if_mine(channel, i, j, lambda: product(channel, i, j))

            if (i, j) == (2, 2) and channel == 1:

                @pl.when(is_end)
                def _():
                    for k, l in [(1, 1), (0, 1)]:
                        if_mine(0, k, l, lambda: stream(outgo_a, from_out, 0, k, l, 0, inner).start())


            if (i, j) in forwards:

                @pl.when(is_middle)
                def _():
                    for way, k, l in forwards[i, j]:
                        if_mine(channel, k, l, lambda: (to_inner if way == "in" else to_outer)(channel, k, l))

    scale = 1.0 / (FRAMES * 2 * CHIPS)

    def swap(channel, block, planes):
        return pltpu.make_async_remote_copy(
            src_ref=stage.at[channel, planes, :, lanes_of(block)],
            dst_ref=arrived.at[channel, planes, :, lanes_of(block)],
            send_sem=half_send.at[channel, block],
            recv_sem=half_recv.at[channel, block],
            device_id=sibling,
            device_id_type=MESH,
        )

    def put(channel, block, plane, value):
        rows_out[:, channel, plane, lanes_of(block)] = value

    own_rows = pl.ds(pl.multiple_of(core * 128, 128), 128)
    other_rows = pl.ds(pl.multiple_of((1 - core) * 128, 128), 128)

    def finish_block(channel, i, j, own_is_row, total):
        rows, columns = actual(i, j)
        if i == j:

            @pl.when(mine(channel, i, j))
            def _():
                packed = total() * scale
                flipped = packed.T
                work[0] = jnp.where(row_id <= col_id, packed, flipped)
                work[1] = jnp.where(row_id > col_id, packed, jnp.where(row_id == col_id, 0.0, -flipped))
                for plane in range(2):
                    stage[channel, plane, :, lanes_of(rows)] = work[plane, other_rows, :]
                swap(channel, rows, pl.ds(0, 2)).start()
                for plane in range(2):
                    put(channel, rows, plane, work[plane, own_rows, :])

        else:
            straight = mirror == (0 if own_is_row else 1)
            block = columns * straight.astype(jnp.int32) + rows * (1 - straight.astype(jnp.int32))

            @pl.when(straight)
            def _():
                work[0] = total() * scale

            @pl.when(jnp.logical_not(straight))
            def _():
                work[0] = total().T * (scale * (1 - 2 * core).astype(F32))

            stage[channel, core, :, lanes_of(block)] = work[0, other_rows, :]
            swap(channel, block, pl.ds(core, 1)).start()
            put(channel, block, core, work[0, own_rows, :])

    def finish(channel):
        @pl.when(is_end)
        def _():
            for i, j in outward:
                slot = slot_of(i, j)

                def wait(i=i, j=j):
                    stream(outgo_b, from_in, channel, i, j, 2, inner).wait_recv()

                if_mine(channel, i, j, wait)
                finish_block(
                    channel, i, j, True, lambda: part[channel, slot] + from_in[channel, slot].astype(F32)
                )

        @pl.when(is_middle)
        def _():
            for i, j in [(1, 3), (1, 2), (1, 1), (0, 1)]:
                slot = slot_of(i, j)

                def wait(i=i, j=j):
                    if j == 1:
                        stream(outgo_a, from_out, channel, i, j, 0, outer).wait_recv()
                    if i == 1:
                        stream(outgo_a, from_in, channel, i, j, 1, inner).wait_recv()

                if_mine(channel, i, j, wait)
                finish_block(
                    channel, i, j, i == 1,
                    lambda: part[channel, slot]
                    + from_out[channel, slot].astype(F32)
                    + from_in[channel, slot].astype(F32),
                )

    def block_copy(channel, block):
        lanes = lanes_of(block)
        return pltpu.make_async_copy(
            rows_out.at[:, channel, :, lanes], vis_out.at[:, channel, :, lanes], out_sem.at[2 + channel]
        )

    def collect(channel):
        for place in (3, 2, 1, 0):
            block = place + mirror * (3 - 2 * place)

            @pl.when(middle != place)
            def _():
                swap(channel, block, pl.ds(1 - core, 1)).wait_recv()
                put(channel, block, 1 - core, arrived[channel, 1 - core, :, lanes_of(block)])

            @pl.when(jnp.logical_and(middle == place, core != (block + channel) % 2))
            def _():
                swap(channel, block, pl.ds(0, 2)).wait_recv()
                for plane in range(2):
                    put(channel, block, plane, arrived[channel, plane, :, lanes_of(block)])

            block_copy(channel, block).start()

    def vis_copy(channel):
        return pltpu.make_async_copy(rows_out.at[:, channel], vis_out.at[:, channel], out_sem.at[2 + channel])

    def drain_spectra():
        @pl.when(ta < 2 * CHIPS - 1)
        def _():
            halo.wait_send()

        for channel in range(2):

            def drain(step, carry, channel=channel):
                to_owner(channel, (col + step) % COLS, pl.ds(0, QF)).wait_send()
                return carry

            lax.fori_loop(1, COLS, drain, 0)
            for copy in pair_copies(channel, pl.ds(0, NIN)):
                copy.wait_send()
            spec_copy(channel).wait()

    def drain_line(channel):
        @pl.when(is_end)
        def _():
            for i, j in ORDER:
                if j >= 1:
                    if_mine(channel, i, j, lambda: stream(outgo_a, from_out, channel, i, j, 0, inner).wait_send())

        @pl.when(is_middle)
        def _():
            for i, j in inward:
                if_mine(channel, i, j, lambda: stream(outgo_a, from_in, channel, i, j, 1, inner).wait_send())
            for i, j in outward:
                if_mine(channel, i, j, lambda: stream(outgo_b, from_in, channel, i, j, 2, outer).wait_send())

        for block in range(CHIPS):

            @pl.when(chip != block)
            def _():
                swap(channel, block, pl.ds(core, 1)).wait_send()

            @pl.when(jnp.logical_and(chip == block, core == (block + channel) % 2))
            def _():
                swap(channel, block, pl.ds(0, 2)).wait_send()

    own.wait()
    gather(0)
    spec_copy(0).start()
    for copy in pair_copies(0, pl.ds(0, NIN)):
        copy.wait_recv()
    products(0)
    gather(1)
    spec_copy(1).start()
    for copy in pair_copies(1, pl.ds(0, NIN)):
        copy.wait_recv()
    products(1)
    finish(0)
    collect(0)
    drain_spectra()
    drain_line(0)
    finish(1)
    collect(1)
    drain_line(1)
    vis_copy(0).wait()
    vis_copy(1).wait()


def body(voltages, taps_filter):
    blocks = (2, len(ORDER), BLK, BLK)
    spectra, visib = pl.pallas_call(
        kernel,
        out_shape=(
            jax.ShapeDtypeStruct((2, 2 * FRAMES, NIN), BF16),
            jax.ShapeDtypeStruct((128, 2, 2, NIN), F32),
        ),
        in_specs=[
            pl.BlockSpec(memory_space=pl.ANY),
            pl.BlockSpec(memory_space=pltpu.VMEM),
        ],
        out_specs=(pl.BlockSpec(memory_space=pl.ANY), pl.BlockSpec(memory_space=pl.ANY)),
        scratch_shapes=[
            pltpu.VMEM((FR, FR), BF16),
            pltpu.VMEM((FRAMES + TAPS, LOCAL, FR), BF16),
            pltpu.VMEM((JC, FR, FR), BF16),
            pltpu.VMEM((JC * FR, FR), F32),
            pltpu.VMEM((FR, QF, FR), BF16),
            pltpu.VMEM((COLS, 4, QF, FR), BF16),
            pltpu.VMEM((2, 2 * FRAMES, NIN), BF16),
            pltpu.VMEM((2, NIN, 4 * FRAMES), BF16),
            pltpu.VMEM((2, 4 * FRAMES, NIN), BF16),
            pltpu.VMEM((2, 2 * FRAMES, NIN), BF16),
            pltpu.VMEM(blocks, F32),
            pltpu.VMEM(blocks, BF16),
            pltpu.VMEM(blocks, BF16),
            pltpu.VMEM(blocks, BF16),
            pltpu.VMEM(blocks, BF16),
            pltpu.VMEM((2, BLK, BLK), F32),
            pltpu.VMEM((2, 2, 128, NIN), F32),
            pltpu.VMEM((2, 2, 128, NIN), F32),
            pltpu.VMEM((128, 2, 2, NIN), F32),
            pltpu.SemaphoreType.DMA((2, 4)),
            pltpu.SemaphoreType.DMA((2,)),
            pltpu.SemaphoreType.DMA((2, COLS)),
            pltpu.SemaphoreType.DMA((2, COLS)),
            pltpu.SemaphoreType.DMA((1,)),
            pltpu.SemaphoreType.DMA((2, 2)),
            pltpu.SemaphoreType.DMA((2, 2)),
            pltpu.SemaphoreType.DMA((2, 3, len(ORDER))),
            pltpu.SemaphoreType.DMA((2, 3, len(ORDER))),
            pltpu.SemaphoreType.DMA((2, CHIPS)),
            pltpu.SemaphoreType.DMA((2, CHIPS)),
            pltpu.SemaphoreType.DMA((4,)),
        ],
        compiler_params=pltpu.CompilerParams(
            collective_id=0, has_side_effects=True, vmem_limit_bytes=48 * 2**20
        ),
        name="correlator",
    )(voltages, taps_filter)
    return spectra.reshape(2, 2, FRAMES, NIN), visib


def solution(mesh):
    return jax.shard_map(
        body,
        mesh=mesh,
        in_specs=(P("ta", "col", None), P()),
        out_specs=(P("col", None, "ta", None), P("ta", "col", None, None)),
        check_vma=False,
    )
```

```python
import jax
import jax.numpy as jnp
import numpy as np
from jax import lax
from jax.experimental import pallas as pl
from jax.experimental.pallas import tpu as pltpu
from jax.sharding import PartitionSpec as P

MESH = pl.DeviceIdType.MESH
F32 = jnp.float32
BF16 = jnp.bfloat16

TAPS = 16
FR = 128
FRAMES = 256
LOCAL = 32
COLS = 32
NIN = 1024
CHIPS = 4
BLK = NIN // CHIPS
QF = FRAMES // 4
JC = 16
NJC = QF // JC
GROUPS = COLS // 4

ORDER = [(0, 3), (1, 3), (2, 3), (3, 3), (0, 2), (1, 2), (2, 2), (1, 1), (0, 1), (0, 0)]


def make_table_rows():
    row = lax.broadcasted_iota(jnp.int32, (FR, FR), 0)
    sample = lax.broadcasted_iota(jnp.int32, (FR, FR), 1)
    phase = ((row // 2) * sample + (row % 2) * (FR // 4)) % FR
    return jnp.cos(phase.astype(F32) * (2.0 * np.pi / FR)).astype(BF16)


def kernel(
    volt, taps, spec_out, vis_out,
    table, padded, filt, wide, sendbuf, recvbuf, spectra, across, right, for_sibling, part, outgo_a, outgo_b, from_out, from_in, work, stage, arrived, rows_out,
    load_sem, halo_sem, a2a_send, a2a_recv, own_sem, pair_send, pair_recv, line_send, line_recv, half_send, half_recv, out_sem,
):
    ta = lax.axis_index("ta")
    col = lax.axis_index("col")
    chip = ta // 2
    core = ta % 2
    mirror = chip // 2
    middle = chip * (1 - mirror) + (3 - chip) * mirror
    inner = {"ta": (chip + 1 - 2 * mirror) * 2 + core, "col": col}
    outer = {"ta": (chip - 1 + 2 * mirror) * 2 + core, "col": col}
    sibling = {"ta": chip * 2 + 1 - core, "col": col}
    before = {"ta": ta - 1, "col": col}
    after = {"ta": ta + 1, "col": col}
    is_end = middle == 0
    is_middle = middle == 1
    cross_after = jnp.logical_and(core == 1, chip < CHIPS - 1)
    cross_before = jnp.logical_and(core == 0, chip > 0)

    def loads(half):
        return [
            pltpu.make_async_copy(
                volt.at[pl.ds(b * QF + half * (QF // 2), QF // 2)],
                padded.at[pl.ds(TAPS + b * QF + half * (QF // 2), QF // 2)],
                load_sem.at[half, b],
            )
            for b in range(4)
        ]

    for half in range(2):
        for load in loads(half):
            load.start()

    barrier = pltpu.get_barrier_semaphore()

    def greet(device):
        pl.semaphore_signal(barrier, inc=1, device_id=device, device_id_type=MESH)

    def greet_col(step, carry):
        greet({"ta": ta, "col": (col + step) % COLS})
        return carry

    lax.fori_loop(1, COLS, greet_col, 0)
    greet(sibling)
    greet(inner)

    @pl.when(is_middle)
    def _():
        greet(outer)

    @pl.when(cross_after)
    def _():
        greet(after)

    @pl.when(cross_before)
    def _():
        greet(before)

    @pl.when(ta == 0)
    def _():
        padded[0:TAPS] = jnp.zeros((TAPS, LOCAL, FR), BF16)

    table[...] = make_table_rows()
    for load in loads(0):
        load.wait()

    def front(chunk):
        def filter_part(step, carry):
            group = step // 2
            rows = pl.ds(pl.multiple_of((step % 2) * 16, 16), 16)
            out_rows = pl.ds(pl.multiple_of(group * LOCAL + (step % 2) * 16, 16), 16)
            weights = [taps[t : t + 1, :] for t in range(TAPS)]
            for part_of in range(JC // 8):
                base = group * QF + chunk * JC + part_of * 8 + 1
                held = [padded[base + i, rows, :].astype(F32) for i in range(TAPS + 7)]
                for o in range(8):
                    total = weights[0] * held[o]
                    for t in range(1, TAPS):
                        total = total + weights[t] * held[o + t]
                    filt[part_of * 8 + o, out_rows, :] = total.astype(BF16)
            return carry

        lax.fori_loop(0, 8, filter_part, 0)
        for j in range(JC):
            wide[pl.ds(j, FR, stride=JC), :] = lax.dot_general(
                table[...], filt[j], (((1,), (1,)), ((), ())), preferred_element_type=F32
            )
        sendbuf[:, pl.ds(chunk * JC, JC), :] = wide[...].reshape(FR, JC, FR).astype(BF16)

    def to_owner(channel, peer, rows):
        return pltpu.make_async_remote_copy(
            src_ref=sendbuf.at[pl.ds(peer * 4 + 2 * channel, 2), rows],
            dst_ref=recvbuf.at[col, pl.ds(2 * channel, 2), rows],
            send_sem=a2a_send.at[channel, peer],
            recv_sem=a2a_recv.at[channel, col],
            device_id={"ta": ta, "col": peer},
            device_id_type=MESH,
        )

    def send_chunk(channel, rows):
        def send_one(step, carry):
            to_owner(channel, (col + step) % COLS, rows).start()
            return carry

        lax.fori_loop(1, COLS, send_one, 0)

    halo = pltpu.make_async_remote_copy(
        src_ref=padded.at[pl.ds(FRAMES, TAPS)],
        dst_ref=padded.at[pl.ds(0, TAPS)],
        send_sem=halo_sem.at[0],
        recv_sem=halo_sem.at[1],
        device_id=after,
        device_id_type=MESH,
    )

    front(1)
    for load in loads(1):
        load.wait()
    pl.semaphore_wait(
        barrier,
        COLS + 1 + middle + cross_after.astype(jnp.int32) + cross_before.astype(jnp.int32),
    )

    @pl.when(ta < 2 * CHIPS - 1)
    def _():
        halo.start()

    send_chunk(0, pl.ds(1 * JC, JC))
    front(2)
    send_chunk(0, pl.ds(2 * JC, JC))
    front(3)
    send_chunk(0, pl.ds(3 * JC, JC))

    @pl.when(ta > 0)
    def _():
        halo.wait_recv()

    front(0)
    send_chunk(0, pl.ds(0 * JC, JC))
    send_chunk(1, pl.ds(0, QF))
    own = pltpu.make_async_copy(sendbuf.at[pl.ds(col * 4, 4)], recvbuf.at[col], own_sem.at[0])
    own.start()

    def pair_copies(channel, lanes):
        own_k, sibling_k = pl.ds(0, 2 * FRAMES), pl.ds(2 * FRAMES, 2 * FRAMES)
        ways = [
            (across.at[channel, lanes, own_k], across.at[channel, lanes, sibling_k]),
            (for_sibling.at[channel, :, lanes], right.at[channel, sibling_k, lanes]),
        ]
        return [
            pltpu.make_async_remote_copy(
                src_ref=src,
                dst_ref=dst,
                send_sem=pair_send.at[channel, way],
                recv_sem=pair_recv.at[channel, way],
                device_id=sibling,
                device_id_type=MESH,
            )
            for way, (src, dst) in enumerate(ways)
        ]

    def gather(channel):
        def regroup_one(g, carry):
            lanes = pl.ds(pl.multiple_of(g * 128, 128), 128)
            for i in range(4):
                source = g * 4 + i

                @pl.when(source != col)
                def _():
                    pltpu.make_async_remote_copy(
                        src_ref=recvbuf.at[source, pl.ds(2 * channel, 2)],
                        dst_ref=recvbuf.at[source, pl.ds(2 * channel, 2)],
                        send_sem=a2a_send.at[channel, source],
                        recv_sem=a2a_recv.at[channel, source],
                        device_id={"ta": ta, "col": source},
                        device_id_type=MESH,
                    ).wait_recv()

            for r in range(2):
                held = [recvbuf[g * 4 + i, 2 * channel + r] for i in range(4)]
                value = jnp.concatenate(
                    [
                        jnp.concatenate([h[:, b * LOCAL : (b + 1) * LOCAL] for h in held], axis=1)
                        for b in range(4)
                    ],
                    axis=0,
                )
                here, there = pl.ds(r * FRAMES, FRAMES), pl.ds((1 - r) * FRAMES, FRAMES)
                spectra[channel, here, lanes] = value
                across[channel, lanes, here] = value.T

                @pl.when(core == 0)
                def _():
                    right[channel, here, lanes] = value
                    for_sibling[channel, there, lanes] = value if r == 1 else -value

                @pl.when(core == 1)
                def _():
                    right[channel, there, lanes] = value if r == 1 else -value
                    for_sibling[channel, here, lanes] = value

            for copy in pair_copies(channel, lanes):
                copy.start()
            return carry

        lax.fori_loop(0, GROUPS, regroup_one, 0)

    def spec_copy(channel):
        return pltpu.make_async_copy(spectra.at[channel], spec_out.at[channel], out_sem.at[channel])

    def actual(i, j):
        return i + mirror * (3 - i - j), j + mirror * (3 - i - j)

    def slot_of(i, j):
        rows, columns = actual(i, j)
        return columns * (columns + 1) // 2 + rows

    def lanes_of(block):
        return pl.ds(pl.multiple_of(block * BLK, BLK), BLK)

    def mine(channel, i, j):
        return None if i != j else core == (i + mirror + channel) % 2

    def if_mine(channel, i, j, run):
        if i == j:
            pl.when(mine(channel, i, j))(run)
        else:
            run()

    def stream(buffer, landing, channel, i, j, way, device):
        slot = slot_of(i, j)
        return pltpu.make_async_remote_copy(
            src_ref=buffer.at[channel, slot],
            dst_ref=landing.at[channel, slot],
            send_sem=line_send.at[channel, way, slot],
            recv_sem=line_recv.at[channel, way, slot],
            device_id=device,
            device_id_type=MESH,
        )


    row_id = lax.broadcasted_iota(jnp.int32, (BLK, BLK), 0)
    col_id = lax.broadcasted_iota(jnp.int32, (BLK, BLK), 1)
    inward = [(i, j) for i, j in ORDER if j >= 2]
    outward = [(0, j) for j in range(CHIPS - 1, -1, -1)]
    forwards = {
        (0, 3): [("in", 0, 3)],
        (1, 3): [("in", 1, 3)],
        (2, 3): [("in", 2, 3)],
        (3, 3): [("in", 3, 3), ("out", 0, 3)],
        (0, 2): [("out", 0, 2)],
        (0, 1): [("out", 0, 1)],
        (0, 0): [("out", 0, 0), ("in", 0, 2), ("in", 1, 2), ("in", 2, 2)],
    }

    def product(channel, i, j):
        rows, columns = actual(i, j)
        slot = slot_of(i, j)
        lhs = across[channel, lanes_of(rows), :]
        value = jnp.dot(lhs, right[channel, :, lanes_of(columns)], preferred_element_type=F32)
        if i == j:
            other = jnp.zeros((BLK, BLK), F32)
            for k in range(4):
                term = jnp.dot(
                    lhs[:, k * FRAMES : (k + 1) * FRAMES],
                    right[channel, (k ^ 1) * FRAMES : ((k ^ 1) + 1) * FRAMES, lanes_of(columns)],
                    preferred_element_type=F32,
                )
                other = other + term if k % 2 == 0 else other - term
            real = jnp.where(core == 0, value, -other)
            imag = jnp.where(core == 0, other, value)
            value = jnp.where(row_id <= col_id, real, imag)
        part[channel, slot] = value
        if j >= 1:

            @pl.when(is_end)
            def _():
                outgo_a[channel, slot] = value.astype(BF16)
                if j >= 2 or channel == 1:
                    stream(outgo_a, from_out, channel, i, j, 0, inner).start()

    def to_inner(channel, i, j):
        slot = slot_of(i, j)
        stream(outgo_a, from_out, channel, i, j, 0, outer).wait_recv()
        outgo_a[channel, slot] = (part[channel, slot] + from_out[channel, slot].astype(F32)).astype(BF16)
        stream(outgo_a, from_in, channel, i, j, 1, inner).start()

    def to_outer(channel, i, j):
        slot = slot_of(i, j)
        stream(outgo_b, from_in, channel, i, j, 1, inner).wait_recv()
        outgo_b[channel, slot] = (part[channel, slot] + from_in[channel, slot].astype(F32)).astype(BF16)
        stream(outgo_b, from_in, channel, i, j, 2, outer).start()

    def products(channel):
        for i, j in ORDER:
            if_mine(channel, i, j, lambda: product(channel, i, j))

            if (i, j) == (2, 2) and channel == 1:

                @pl.when(is_end)
                def _():
                    for k, l in [(1, 1), (0, 1)]:
                        if_mine(0, k, l, lambda: stream(outgo_a, from_out, 0, k, l, 0, inner).start())


            if (i, j) in forwards:

                @pl.when(is_middle)
                def _():
                    for way, k, l in forwards[i, j]:
                        if_mine(channel, k, l, lambda: (to_inner if way == "in" else to_outer)(channel, k, l))

    scale = 1.0 / (FRAMES * 2 * CHIPS)

    def swap(channel, block, planes):
        return pltpu.make_async_remote_copy(
            src_ref=stage.at[channel, planes, :, lanes_of(block)],
            dst_ref=arrived.at[channel, planes, :, lanes_of(block)],
            send_sem=half_send.at[channel, block],
            recv_sem=half_recv.at[channel, block],
            device_id=sibling,
            device_id_type=MESH,
        )

    def put(channel, block, plane, value):
        rows_out[:, channel, plane, lanes_of(block)] = value

    own_rows = pl.ds(pl.multiple_of(core * 128, 128), 128)
    other_rows = pl.ds(pl.multiple_of((1 - core) * 128, 128), 128)

    def finish_block(channel, i, j, own_is_row, total):
        rows, columns = actual(i, j)
        if i == j:

            @pl.when(mine(channel, i, j))
            def _():
                packed = total() * scale
                flipped = packed.T
                work[0] = jnp.where(row_id <= col_id, packed, flipped)
                work[1] = jnp.where(row_id > col_id, packed, jnp.where(row_id == col_id, 0.0, -flipped))
                for plane in range(2):
                    stage[channel, plane, :, lanes_of(rows)] = work[plane, other_rows, :]
                swap(channel, rows, pl.ds(0, 2)).start()
                for plane in range(2):
                    put(channel, rows, plane, work[plane, own_rows, :])

        else:
            straight = mirror == (0 if own_is_row else 1)
            block = columns * straight.astype(jnp.int32) + rows * (1 - straight.astype(jnp.int32))

            @pl.when(straight)
            def _():
                work[0] = total() * scale

            @pl.when(jnp.logical_not(straight))
            def _():
                work[0] = total().T * (scale * (1 - 2 * core).astype(F32))

            stage[channel, core, :, lanes_of(block)] = work[0, other_rows, :]
            swap(channel, block, pl.ds(core, 1)).start()
            put(channel, block, core, work[0, own_rows, :])

    def finish(channel):
        @pl.when(is_end)
        def _():
            for i, j in outward:
                slot = slot_of(i, j)

                def wait(i=i, j=j):
                    stream(outgo_b, from_in, channel, i, j, 2, inner).wait_recv()

                if_mine(channel, i, j, wait)
                finish_block(
                    channel, i, j, True, lambda: part[channel, slot] + from_in[channel, slot].astype(F32)
                )

        @pl.when(is_middle)
        def _():
            for i, j in [(1, 3), (1, 2), (1, 1), (0, 1)]:
                slot = slot_of(i, j)

                def wait(i=i, j=j):
                    if j == 1:
                        stream(outgo_a, from_out, channel, i, j, 0, outer).wait_recv()
                    if i == 1:
                        stream(outgo_a, from_in, channel, i, j, 1, inner).wait_recv()

                if_mine(channel, i, j, wait)
                finish_block(
                    channel, i, j, i == 1,
                    lambda: part[channel, slot]
                    + from_out[channel, slot].astype(F32)
                    + from_in[channel, slot].astype(F32),
                )

    def block_copy(channel, block):
        lanes = lanes_of(block)
        return pltpu.make_async_copy(
            rows_out.at[:, channel, :, lanes], vis_out.at[:, channel, :, lanes], out_sem.at[2 + channel]
        )

    def collect(channel):
        for place in (3, 2, 1, 0):
            block = place + mirror * (3 - 2 * place)

            @pl.when(middle != place)
            def _():
                swap(channel, block, pl.ds(1 - core, 1)).wait_recv()
                put(channel, block, 1 - core, arrived[channel, 1 - core, :, lanes_of(block)])

            @pl.when(jnp.logical_and(middle == place, core != (block + channel) % 2))
            def _():
                swap(channel, block, pl.ds(0, 2)).wait_recv()
                for plane in range(2):
                    put(channel, block, plane, arrived[channel, plane, :, lanes_of(block)])

            block_copy(channel, block).start()

    def vis_copy(channel):
        return pltpu.make_async_copy(rows_out.at[:, channel], vis_out.at[:, channel], out_sem.at[2 + channel])

    def drain_spectra():
        @pl.when(ta < 2 * CHIPS - 1)
        def _():
            halo.wait_send()

        for channel in range(2):

            def drain(step, carry, channel=channel):
                to_owner(channel, (col + step) % COLS, pl.ds(0, QF)).wait_send()
                return carry

            lax.fori_loop(1, COLS, drain, 0)
            for copy in pair_copies(channel, pl.ds(0, NIN)):
                copy.wait_send()
            spec_copy(channel).wait()

    def drain_middle(channel):
        @pl.when(is_middle)
        def _():
            for i, j in inward:
                if_mine(channel, i, j, lambda: stream(outgo_a, from_in, channel, i, j, 1, inner).wait_send())
            for i, j in outward:
                if_mine(channel, i, j, lambda: stream(outgo_b, from_in, channel, i, j, 2, outer).wait_send())

    def drain_line(channel):
        @pl.when(is_end)
        def _():
            for i, j in ORDER:
                if j >= 1:
                    if_mine(channel, i, j, lambda: stream(outgo_a, from_out, channel, i, j, 0, inner).wait_send())

        for block in range(CHIPS):

            @pl.when(chip != block)
            def _():
                swap(channel, block, pl.ds(core, 1)).wait_send()

            @pl.when(jnp.logical_and(chip == block, core == (block + channel) % 2))
            def _():
                swap(channel, block, pl.ds(0, 2)).wait_send()

    own.wait()
    gather(0)
    spec_copy(0).start()
    for copy in pair_copies(0, pl.ds(0, NIN)):
        copy.wait_recv()
    products(0)
    gather(1)
    spec_copy(1).start()
    for copy in pair_copies(1, pl.ds(0, NIN)):
        copy.wait_recv()
    products(1)
    finish(0)
    collect(0)
    drain_spectra()
    drain_line(0)
    drain_middle(0)
    drain_middle(1)
    finish(1)
    collect(1)
    drain_line(1)
    vis_copy(0).wait()
    vis_copy(1).wait()


def body(voltages, taps_filter):
    blocks = (2, len(ORDER), BLK, BLK)
    spectra, visib = pl.pallas_call(
        kernel,
        out_shape=(
            jax.ShapeDtypeStruct((2, 2 * FRAMES, NIN), BF16),
            jax.ShapeDtypeStruct((128, 2, 2, NIN), F32),
        ),
        in_specs=[
            pl.BlockSpec(memory_space=pl.ANY),
            pl.BlockSpec(memory_space=pltpu.VMEM),
        ],
        out_specs=(pl.BlockSpec(memory_space=pl.ANY), pl.BlockSpec(memory_space=pl.ANY)),
        scratch_shapes=[
            pltpu.VMEM((FR, FR), BF16),
            pltpu.VMEM((FRAMES + TAPS, LOCAL, FR), BF16),
            pltpu.VMEM((JC, FR, FR), BF16),
            pltpu.VMEM((JC * FR, FR), F32),
            pltpu.VMEM((FR, QF, FR), BF16),
            pltpu.VMEM((COLS, 4, QF, FR), BF16),
            pltpu.VMEM((2, 2 * FRAMES, NIN), BF16),
            pltpu.VMEM((2, NIN, 4 * FRAMES), BF16),
            pltpu.VMEM((2, 4 * FRAMES, NIN), BF16),
            pltpu.VMEM((2, 2 * FRAMES, NIN), BF16),
            pltpu.VMEM(blocks, F32),
            pltpu.VMEM(blocks, BF16),
            pltpu.VMEM(blocks, BF16),
            pltpu.VMEM(blocks, BF16),
            pltpu.VMEM(blocks, BF16),
            pltpu.VMEM((2, BLK, BLK), F32),
            pltpu.VMEM((2, 2, 128, NIN), F32),
            pltpu.VMEM((2, 2, 128, NIN), F32),
            pltpu.VMEM((128, 2, 2, NIN), F32),
            pltpu.SemaphoreType.DMA((2, 4)),
            pltpu.SemaphoreType.DMA((2,)),
            pltpu.SemaphoreType.DMA((2, COLS)),
            pltpu.SemaphoreType.DMA((2, COLS)),
            pltpu.SemaphoreType.DMA((1,)),
            pltpu.SemaphoreType.DMA((2, 2)),
            pltpu.SemaphoreType.DMA((2, 2)),
            pltpu.SemaphoreType.DMA((2, 3, len(ORDER))),
            pltpu.SemaphoreType.DMA((2, 3, len(ORDER))),
            pltpu.SemaphoreType.DMA((2, CHIPS)),
            pltpu.SemaphoreType.DMA((2, CHIPS)),
            pltpu.SemaphoreType.DMA((4,)),
        ],
        compiler_params=pltpu.CompilerParams(
            collective_id=0, has_side_effects=True, vmem_limit_bytes=48 * 2**20
        ),
        name="correlator",
    )(voltages, taps_filter)
    return spectra.reshape(2, 2, FRAMES, NIN), visib


def solution(mesh):
    return jax.shard_map(
        body,
        mesh=mesh,
        in_specs=(P("ta", "col", None), P()),
        out_specs=(P("col", None, "ta", None), P("ta", "col", None, None)),
        check_vma=False,
    )
```
